128 devices in a mesh: owner: 8 (over y, core), tile: 16 (over z, x).
Axes of the slice: x: 4, y: 4, z: 4, core: 2. Of those that a mesh axis runs over, the one named last changes fastest.
Arguments:
- embeddings: bfloat16 [131072, 1024], P(('owner', 'tile')), may hold values from -40 to 40, as said below
- sorted_pos: int32 [131072], P(('owner', 'tile')), may hold values from 0 to 131071, as said below
- block_cluster: int32 [1024], P(('owner', 'tile')), may hold values from 0 to 63, as said below
- tile_list: int32 [8, 16, 2, 8320], P('owner', 'tile'), may hold values from -1 to 127, as said below
Outputs:
- max_sim: float32 [131072], P(('owner', 'tile'))
The draws below stay inside these ranges and needn't reach their ends.
Inputs may be any that keep to these rules, and one draw needn't show every extreme that they name: Raw embeddings with row scales within a factor of ten. `sorted_pos`: A permutation; the rows of each device go to exactly 8 positions in each device's range of 1024 cluster-order positions. `block_cluster`: never falling; each cluster is a run of whole blocks inside one group of 128 blocks (the blocks held by one index of owner), and group g holds exactly the clusters g * 8 to (g + 1) * 8 - 1. `tile_list`: over the workers of one group, every pair rb >= cb of the group's blocks in one cluster is listed exactly once; unused entries are -1 in both places and follow a worker's used ones; workers' lists differ in length.
All inputs are finite; a program needn't handle non-finite values.
Results may differ from the reference program's by a relative error of at most 0.0005.
Values may be sent and summed in bfloat16 or wider, within the bound.
A program may use at most 192 MiB of HBM per device.

```python
import jax
import jax.numpy as jnp
from jax import lax

D = 1024
BLK = 128
ROW_DEV = 1024
CL_GRP = 8
ROWS = 131072
GRP_BLK = 128
NBLK = 1024
PAIR = 8
TPW = 8320
N_OWNER = 8
N_TILE = 16


def group_layout(group_key):
    first, second, third = jax.random.split(group_key, 3)
    giant = jax.random.randint(first, (), GRP_BLK // 2, 3 * GRP_BLK // 4 + 1)
    places = jnp.arange(GRP_BLK, dtype=jnp.int32)
    scores = jax.random.randint(second, (GRP_BLK,), 0, 1 << 20) * GRP_BLK + places
    scores = jnp.where(places > giant, scores, -1)
    starts = lax.top_k(scores, CL_GRP - 2)[0] % GRP_BLK
    local = (places >= giant).astype(jnp.int32) + jnp.sum((places[:, None] >= starts[None, :]).astype(jnp.int32), axis=1)
    shifted = jax.random.randint(third, (), 0, N_TILE)
    return (local.astype(jnp.int32), shifted.astype(jnp.int32))


def layouts(key):
    group_keys = jax.vmap(lambda group: jax.random.fold_in(key, group))(jnp.arange(N_OWNER))
    return jax.vmap(group_layout)(group_keys)


def group_lists(local, shifted):
    places = jnp.arange(GRP_BLK, dtype=jnp.int32)
    row_grid = jnp.broadcast_to(places[:, None], (GRP_BLK, GRP_BLK))
    col_grid = jnp.broadcast_to(places[None, :], (GRP_BLK, GRP_BLK))
    usable = (col_grid <= row_grid) & (local[:, None] == local[None, :])
    worker = (shifted + 8 * local[:, None] + row_grid % 8) % N_TILE
    usable_flat = usable.reshape(-1)
    worker_flat = worker.reshape(-1)
    onehot = ((worker_flat[:, None] == jnp.arange(N_TILE, dtype=jnp.int32)[None, :]) & usable_flat[:, None]).astype(jnp.int32)
    placed = jnp.sum((jnp.cumsum(onehot, axis=0) - 1) * onehot, axis=1)
    target = jnp.where(usable_flat, worker_flat * TPW + placed, N_TILE * TPW)
    table = jnp.full((2, N_TILE * TPW + 1), -1, jnp.int32)
    table = table.at[0, target].set(row_grid.reshape(-1)).at[1, target].set(col_grid.reshape(-1))
    return table[:, :N_TILE * TPW].reshape(2, N_TILE, TPW).transpose(1, 0, 2)


def draw_block_cluster(key, part):
    local, shifted = layouts(key)
    return (local + CL_GRP * jnp.arange(N_OWNER, dtype=jnp.int32)[:, None]).reshape(N_OWNER * GRP_BLK).astype(jnp.int32)


def draw_tile_list(key, part):
    local, shifted = layouts(key)
    return jax.vmap(group_lists)(local, shifted).astype(jnp.int32)


def draw_sorted_pos(key, part):
    key = jax.random.fold_in(key, 9)
    devices_all = N_OWNER * N_TILE
    first, second = jax.random.split(key)
    source_perm = jax.vmap(lambda inner_key: jax.random.permutation(inner_key, ROW_DEV))(jax.random.split(first, devices_all)).astype(jnp.int32)
    target_perm = jax.vmap(lambda inner_key: jax.random.permutation(inner_key, ROW_DEV))(jax.random.split(second, devices_all)).astype(jnp.int32)
    target = source_perm // PAIR
    within = source_perm % PAIR
    source = jnp.arange(devices_all, dtype=jnp.int32)[:, None]
    landing = target_perm[target, source * PAIR + within]
    return (target * ROW_DEV + landing).reshape(-1).astype(jnp.int32)


def draw_embeddings(key, part):
    key = jax.random.fold_in(key, 3)
    first, second, third = jax.random.split(key, 3)
    common = jax.random.normal(first, (D,), jnp.float32)
    row_scale = jnp.exp(jax.random.uniform(third, (ROWS, 1), jnp.float32, 0.0, 2.302585))
    noise = jax.random.normal(second, (ROWS, D), jnp.float32)
    mixing = 0.9
    return jnp.clip(row_scale * (mixing * common[None, :] + noise), -40.0, 40.0).astype(jnp.bfloat16)


def setup_inputs(seed: int = 0) -> dict:
    seeds = jax.random.split(jax.random.key(seed), 5)
    embeddings = draw_embeddings(jax.random.fold_in(seeds[4], 71), 0)
    sorted_pos = draw_sorted_pos(jax.random.fold_in(seeds[4], 71), 0)
    block_cluster = draw_block_cluster(jax.random.fold_in(seeds[4], 71), 0)
    tile_list = draw_tile_list(jax.random.fold_in(seeds[4], 71), 0)
    return {"embeddings": embeddings, "sorted_pos": sorted_pos, "block_cluster": block_cluster, "tile_list": tile_list}


def reference(embeddings, sorted_pos, block_cluster, tile_list):
    values = embeddings.astype(jnp.float32)
    unit = (values * lax.rsqrt(lax.optimization_barrier(jnp.sum(values * values, axis=1, keepdims=True)) + 1e-06)).astype(jnp.bfloat16)
    ordered = jnp.zeros_like(unit).at[sorted_pos].set(unit)
    blocks = ordered.reshape(NBLK, BLK, D)
    offset = (jnp.arange(N_OWNER, dtype=jnp.int32) * GRP_BLK)[:, None, None]
    usable = tile_list[:, :, 0, :] >= 0
    row_blocks = jnp.where(usable, tile_list[:, :, 0, :] + offset, 0).reshape(-1).astype(jnp.int32)
    col_blocks = jnp.where(usable, tile_list[:, :, 1, :] + offset, 0).reshape(-1).astype(jnp.int32)
    ranked = jnp.argsort(jnp.logical_not(usable).reshape(-1).astype(jnp.int32), stable=True).astype(jnp.int32)
    total = jnp.sum(usable.astype(jnp.int32))
    row_blocks = row_blocks[ranked]
    col_blocks = col_blocks[ranked]
    entries = row_blocks.shape[0]
    inner = jnp.arange(BLK, dtype=jnp.int32)
    lanes = jnp.arange(64, dtype=jnp.int32)

    def advance(step, best):
        wanted = step * 64 + lanes
        active = wanted < total
        chosen = jnp.minimum(wanted, entries - 1)
        row_ids = row_blocks[chosen]
        col_ids = col_blocks[chosen]
        queries = blocks[row_ids].astype(jnp.float32)
        columns = blocks[col_ids].astype(jnp.float32)
        scores = jnp.einsum('tid,tjd->tij', queries, columns, precision=lax.Precision.HIGHEST)
        row_at = row_ids[:, None] * BLK + inner[None, :]
        col_at = col_ids[:, None] * BLK + inner[None, :]
        same = block_cluster[row_ids] == block_cluster[col_ids]
        counted = (active & same)[:, None, None] & (col_at[:, None, :] < row_at[:, :, None])
        highest = lax.optimization_barrier(jnp.max(jnp.where(counted, scores, -1.0), axis=2))
        return best.at[row_ids].max(highest)
    best = lax.fori_loop(0, (total + 63) // 64, advance, jnp.full((NBLK, BLK), -1.0, jnp.float32))
    return best.reshape(-1)[sorted_pos]
```

```python
import functools

import jax
import jax.numpy as jnp
from jax import lax
from jax.experimental import pallas as pl
from jax.experimental.pallas import tpu as pltpu
from jax.sharding import PartitionSpec as P

D = 1024
BLK = 128
ROWS = 1024
DEVS = 128
PAIR = ROWS // DEVS
WIDE = D + 128
CHUNK = 256
CHUNKS = ROWS // CHUNK
SLOTS = 6
F32 = jnp.float32
BF16 = jnp.bfloat16
MESH = pl.DeviceIdType.MESH
NT = (((1,), (1,)), ((), ()))
HIGH = lax.Precision.HIGHEST


def place(part):
    core = part // 64
    y = (2 * ((part // 32) % 2) + (part // 2) % 2 + core) % 4
    z = (2 * ((part // 16) % 2) + part % 2 + core) % 4
    x = (part // 4) % 4
    return y * 2 + core, z * 4 + x


def part_of(owner, tile):
    core = owner % 2
    y = (owner // 2 + 4 - core) % 4
    z = (tile // 4 + 4 - core) % 4
    x = tile % 4
    return core * 64 + (y // 2) * 32 + (z // 2) * 16 + x * 4 + (y % 2) * 2 + z % 2


def iota(shape, dim):
    return lax.broadcasted_iota(jnp.int32, shape, dim)


def column(row):
    return jnp.broadcast_to(row, (128, row.shape[1])).T


def kernel(
    x_ref,
    pos_ref,
    bc_ref,
    out_ref,
    unit,
    posc,
    send,
    recv,
    parts,
    bc_here,
    bc_got,
    pos_row,
    clr,
    clc,
    acc,
    acc_got,
    ret_send,
    ret_got,
    rank_ref,
    send_sem,
    recv_sem,
    bc_sem,
    copy_send,
    copy_recv,
    cl_send,
    cl_recv,
    acc_send,
    acc_recv,
    ret_sems,
    local_sem,
):
    owner, tile = lax.axis_index("owner"), lax.axis_index("tile")
    me = part_of(owner, tile)
    core = owner % 2
    x = (me // 4) % 4
    q = me % 4
    base = me - me % 16
    barrier = pltpu.get_barrier_semaphore()

    @pl.loop(1, DEVS)
    def _(k):
        o, t = place((me + k) % DEVS)
        pl.semaphore_signal(barrier, inc=1, device_id=(o, t), device_id_type=MESH)

    pos = pos_ref[...]
    posf = pos.astype(F32)
    posc[...] = column(posf)
    for t in range(ROWS // 128):
        here = posf[:, t * 128 : (t + 1) * 128]
        less = jnp.where(posc[...] < here, 1.0, 0.0)
        rank_ref[:, t * 128 : (t + 1) * 128] = jnp.sum(less, axis=0, keepdims=True).astype(jnp.int32)

    @pl.loop(0, ROWS // 128)
    def _(c):
        rows = pl.ds(pl.multiple_of(c * 128, 128), 128)
        v = x_ref[rows, :].astype(F32)
        s = lax.rsqrt(jnp.sum(v * v, axis=1, keepdims=True) + 1e-06)
        unit[rows, :D] = (v * s).astype(BF16)
        inside = posc[rows, :].astype(jnp.int32) % ROWS
        lane = iota((128, 128), 1)
        meta = jnp.where(lane == 0, inside // 32, jnp.where(lane == 1, inside % 32, 0))
        unit[rows, D:] = meta.astype(F32).astype(BF16)

    @pl.loop(0, CHUNKS)
    def _(c):
        pick = jnp.where(rank_ref[...] == iota((CHUNK, ROWS), 0) + c * CHUNK, 1.0, 0.0).astype(BF16)
        got = jnp.dot(pick, unit[...], preferred_element_type=F32)
        blocks = CHUNK // PAIR
        send[pl.ds(c * blocks, blocks)] = got.reshape(blocks, PAIR, WIDE).astype(BF16)

    for b in range(ROWS // BLK):
        bc_here[b : b + 1, :] = jnp.full((1, 128), bc_ref[b], jnp.int32).astype(F32)

    pl.semaphore_wait(barrier, DEVS - 1)

    listed = owner * 16 + tile

    @pl.when(listed != me)
    def _():
        pltpu.make_async_remote_copy(
            bc_here, bc_got, bc_sem.at[0], bc_sem.at[1], device_id=place(listed), device_id_type=MESH
        ).start()

    @pl.when(listed == me)
    def _():
        pltpu.make_async_copy(bc_here, bc_got, bc_sem.at[1]).start()

    own = pltpu.make_async_copy(send.at[me], recv.at[me], local_sem)
    own.start()

    @pl.loop(1, DEVS)
    def _(k):
        to = (me + k * 37) % DEVS
        pltpu.make_async_remote_copy(
            send.at[to], recv.at[me], send_sem, recv_sem, device_id=place(to), device_id_type=MESH
        ).start()

    pltpu.make_async_copy(bc_here, bc_got, bc_sem.at[1]).wait()

    @pl.when(listed != me)
    def _():
        pltpu.make_async_copy(bc_here, bc_got, bc_sem.at[0]).wait()

    own.wait()
    pltpu.make_async_copy(send.at[pl.ds(0, DEVS - 1)], recv.at[pl.ds(0, DEVS - 1)], recv_sem).wait()

    step = jnp.where(core == 0, 1, 3)
    back = base + ((x + 4 - step) % 4) * 4 + q
    back2 = base + ((x + 2) % 4) * 4 + q
    ahead = base + ((x + step) % 4) * 4 + q
    flip_y = me - q + (q + 2) % 4
    flip_z = me - q + (q // 2) * 2 + (q + 1) % 2
    flip_yz = me - q + 3 - q

    def part_copy(src, c, dst, to):
        rows = pl.ds(c * CHUNK, CHUNK)
        return pltpu.make_async_remote_copy(
            parts.at[src, rows],
            parts.at[dst, rows],
            copy_send.at[dst, c],
            copy_recv.at[dst, c],
            device_id=place(to),
            device_id_type=MESH,
        )

    def arrived(slot, c):
        rows = pl.ds(c * CHUNK, CHUNK)
        pltpu.make_async_copy(parts.at[slot, rows], parts.at[slot, rows], copy_recv.at[slot, c]).wait()

    for c in range(CHUNKS):
        rows = pl.ds(c * CHUNK, CHUNK)
        blocks = CHUNK // PAIR
        parts[0, rows, :] = (
            recv[pl.ds(c * blocks, blocks), :, :D].astype(F32).reshape(CHUNK, D).astype(BF16)
        )
        for dst, to in ((1, back), (3, flip_y), (4, flip_z)):
            part_copy(0, c, dst, to).start()
        meta = recv[pl.ds(c * blocks, blocks), :, D:].astype(F32).reshape(CHUNK, 128).T
        pos_row[:, rows] = jnp.broadcast_to(meta[0:1] * 32.0 + meta[1:2], (8, CHUNK))

    inside = pos_row[...].astype(jnp.int32) // BLK
    own_cl = jnp.zeros((1, ROWS), F32)
    for b in range(ROWS // BLK):
        own_cl = own_cl + jnp.where(inside[0:1] == b, bc_got[b : b + 1, 0:1], 0.0)
    clr[0] = jnp.broadcast_to(own_cl, (8, ROWS))
    for dst, to in ((1, back), (2, back2), (3, flip_y), (4, flip_z), (5, flip_yz)):
        pltpu.make_async_remote_copy(
            clr.at[0], clr.at[dst], cl_send.at[dst], cl_recv.at[dst], device_id=place(to), device_id_type=MESH
        ).start()
    clc[0] = column(own_cl)
    posc[...] = column(pos_row[0:1])
    for m in range(SLOTS):
        acc[m] = jnp.full((8, ROWS), -1.0, F32)

    def fold(s, mask, hi, cols):
        kept = jnp.where(mask, s, -1.0)
        top = jnp.max(kept.reshape(kept.shape[0] // 8, 8, kept.shape[1]), axis=0)
        acc[hi, :, cols] = jnp.maximum(acc[hi, :, cols], top)

    def half_pair(lo, hi, h, n, diag=False):
        rows = pl.ds(pl.multiple_of(h * 512, 512), 512)
        cols = pl.ds(pl.multiple_of(n * CHUNK, CHUNK), CHUNK)
        s = lax.dot_general(parts[lo, rows, :], parts[hi, cols, :], NT, preferred_element_type=F32)
        for half in range(CHUNK // 128):
            at = pl.ds(pl.multiple_of(n * CHUNK + half * 128, 128), 128)
            mask = clc[lo, rows, :] == clr[hi, 0:1, at]
            if diag:
                mask = mask & (posc[rows, :] < pos_row[0:1, at])
            fold(s[:, half * 128 : (half + 1) * 128], mask, hi, at)

    def cl_arrived(slot):
        pltpu.make_async_copy(clr.at[slot], clr.at[slot], cl_recv.at[slot]).wait()
        clc[slot] = column(clr[slot, 0:1])

    @pl.loop(0, 2 * CHUNKS)
    def _(i):
        half_pair(0, 0, i % 2, i // 2, diag=True)

    for slot in (1, 3, 4, 5, 2):
        cl_arrived(slot)

    for c in range(CHUNKS):
        arrived(1, c)
        part_copy(1, c, 2, back).start()
        arrived(3, c)
        if c < CHUNKS // 2:
            part_copy(3, c, 5, flip_z).start()
        arrived(4, c)
        if c >= CHUNKS // 2:
            part_copy(4, c, 5, flip_y).start()

    ahead_hi = (x + step) % 4 > x

    def with_ahead(face):
        lo = jnp.where(ahead_hi, face, 1)
        hi = jnp.where(ahead_hi, 1, face)

        @pl.loop(0, 2 * CHUNKS)
        def _(i):
            half_pair(lo, hi, i % 2, i // 2)

    def with_own(slot, mine_lo):
        lo = jnp.where(mine_lo, 0, slot)
        hi = jnp.where(mine_lo, slot, 0)
        h = jnp.where(mine_lo, 0, 1)

        @pl.loop(0, CHUNKS)
        def _(n):
            half_pair(lo, hi, h, n)

    with_ahead(0)
    with_ahead(3)
    with_ahead(4)
    with_own(3, flip_y > me)
    with_own(4, flip_z > me)
    for c in range(CHUNKS):
        arrived(5, c)
    with_ahead(5)
    with_own(5, flip_yz > me)
    for c in range(CHUNKS):
        arrived(2, c)
    low = x < 2

    @pl.loop(0, CHUNKS)
    def _(n):
        for face in (0, 3, 4, 5):
            half_pair(jnp.where(low, face, 2), jnp.where(low, 2, face), jnp.where(low, 0, 1), n)

    for dst, to in ((1, ahead), (2, back2), (3, flip_y), (4, flip_z), (5, flip_yz)):
        pltpu.make_async_remote_copy(
            acc.at[dst],
            acc_got.at[dst - 1],
            acc_send.at[dst],
            acc_recv.at[dst],
            device_id=place(to),
            device_id_type=MESH,
        ).start()
    best = acc[0]
    for m in range(1, SLOTS):
        pltpu.make_async_copy(acc_got.at[m - 1], acc_got.at[m - 1], acc_recv.at[m]).wait()
        best = jnp.maximum(best, acc_got[m - 1])
    best = jnp.max(best, axis=0, keepdims=True)

    spread = jnp.where(iota((DEVS, ROWS), 1) // PAIR == iota((DEVS, ROWS), 0), best, 0.0)
    fold8 = jnp.where(iota((ROWS, 128), 0) % PAIR == iota((ROWS, 128), 1), 1.0, 0.0)
    ret = jnp.dot(spread, fold8, precision=HIGH, preferred_element_type=F32)
    ret_send[...] = ret.reshape(DEVS, 1, 128)
    back_own = pltpu.make_async_copy(ret_send.at[me], ret_got.at[me], local_sem)
    back_own.start()

    @pl.loop(1, DEVS)
    def _(k):
        to = (me + k * 37) % DEVS
        pltpu.make_async_remote_copy(
            ret_send.at[to],
            ret_got.at[me],
            ret_sems.at[0],
            ret_sems.at[1],
            device_id=place(to),
            device_id_type=MESH,
        ).start()

    back_own.wait()
    most = pl.ds(0, DEVS - 1)
    pltpu.make_async_copy(ret_send.at[most], ret_got.at[most], ret_sems.at[1]).wait()
    got = ret_got[...].reshape(DEVS, 128)
    rank = rank_ref[...]
    turn = jnp.where(rank % PAIR == iota((128, ROWS), 0), 1.0, 0.0)
    rows = jnp.dot(got, turn, precision=HIGH, preferred_element_type=F32)
    out_ref[...] = jnp.sum(
        jnp.where(rank // PAIR == iota((DEVS, ROWS), 0), rows, 0.0), axis=0, keepdims=True
    )

    pltpu.make_async_copy(send.at[most], recv.at[most], send_sem).wait()
    pltpu.make_async_copy(ret_send.at[most], ret_got.at[most], ret_sems.at[0]).wait()
    for c in range(CHUNKS):
        rows = pl.ds(c * CHUNK, CHUNK)
        for dst in range(1, SLOTS):
            pltpu.make_async_copy(parts.at[0, rows], parts.at[dst, rows], copy_send.at[dst, c]).wait()
    for dst in range(1, SLOTS):
        pltpu.make_async_copy(clr.at[0], clr.at[dst], cl_send.at[dst]).wait()
        pltpu.make_async_copy(acc.at[dst], acc_got.at[dst - 1], acc_send.at[dst]).wait()


def per_device(embeddings, sorted_pos, block_cluster, tile_list):
    del tile_list
    vmem = pl.BlockSpec(memory_space=pltpu.VMEM)
    out = pl.pallas_call(
        kernel,
        out_shape=jax.ShapeDtypeStruct((1, ROWS), F32),
        in_specs=[vmem, vmem, pl.BlockSpec(memory_space=pltpu.SMEM)],
        out_specs=vmem,
        scratch_shapes=[
            pltpu.VMEM((ROWS, WIDE), BF16),
            pltpu.VMEM((ROWS, 128), F32),
            pltpu.VMEM((DEVS, PAIR, WIDE), BF16),
            pltpu.VMEM((DEVS, PAIR, WIDE), BF16),
            pltpu.VMEM((SLOTS, ROWS, D), BF16),
            pltpu.VMEM((8, 128), F32),
            pltpu.VMEM((8, 128), F32),
            pltpu.VMEM((8, ROWS), F32),
            pltpu.VMEM((SLOTS, 8, ROWS), F32),
            pltpu.VMEM((SLOTS, ROWS, 128), F32),
            pltpu.VMEM((SLOTS, 8, ROWS), F32),
            pltpu.VMEM((SLOTS - 1, 8, ROWS), F32),
            pltpu.VMEM((DEVS, 1, 128), F32),
            pltpu.VMEM((DEVS, 1, 128), F32),
            pltpu.VMEM((1, ROWS), jnp.int32),
            pltpu.SemaphoreType.DMA,
            pltpu.SemaphoreType.DMA,
            pltpu.SemaphoreType.DMA((2,)),
            pltpu.SemaphoreType.DMA((SLOTS, CHUNKS)),
            pltpu.SemaphoreType.DMA((SLOTS, CHUNKS)),
            pltpu.SemaphoreType.DMA((SLOTS,)),
            pltpu.SemaphoreType.DMA((SLOTS,)),
            pltpu.SemaphoreType.DMA((SLOTS,)),
            pltpu.SemaphoreType.DMA((SLOTS,)),
            pltpu.SemaphoreType.DMA((2,)),
            pltpu.SemaphoreType.DMA,
        ],
        compiler_params=pltpu.CompilerParams(
            collective_id=0, has_side_effects=True, vmem_limit_bytes=56 * 1024 * 1024
        ),
    )(embeddings, sorted_pos.reshape(1, ROWS), block_cluster)
    return out.reshape(ROWS)


def solution(mesh):
    placed = (
        P(("owner", "tile"), None),
        P(("owner", "tile")),
        P(("owner", "tile")),
        P("owner", "tile", None, None),
    )
    return jax.shard_map(
        per_device, mesh=mesh, in_specs=placed, out_specs=P(("owner", "tile")), check_vma=False
    )
```

```python
import functools

import jax
import jax.numpy as jnp
from jax import lax
from jax.experimental import pallas as pl
from jax.experimental.pallas import tpu as pltpu
from jax.sharding import PartitionSpec as P

D = 1024
BLK = 128
ROWS = 1024
DEVS = 128
PAIR = ROWS // DEVS
CHUNK = 256
CHUNKS = ROWS // CHUNK
SLOTS = 6
F32 = jnp.float32
BF16 = jnp.bfloat16
MESH = pl.DeviceIdType.MESH
NT = (((1,), (1,)), ((), ()))
HIGH = lax.Precision.HIGHEST


def place(part):
    core = part // 64
    y = (2 * ((part // 32) % 2) + (part // 2) % 2 + core) % 4
    z = (2 * ((part // 16) % 2) + part % 2 + core) % 4
    x = (part // 4) % 4
    return y * 2 + core, z * 4 + x


def part_of(owner, tile):
    core = owner % 2
    y = (owner // 2 + 4 - core) % 4
    z = (tile // 4 + 4 - core) % 4
    x = tile % 4
    return core * 64 + (y // 2) * 32 + (z // 2) * 16 + x * 4 + (y % 2) * 2 + z % 2


def all_to_all(src, dst, me, core, y, z, x, send_sem, recv_sem):
    rows = [(core + d) % 2 for d in range(2)]
    ys = [(y + d) % 4 for d in range(4)]
    zs = [(z + d) % 4 for d in range(4)]
    xs = [(x + d) % 4 for d in range(4)]
    for k in range(1, DEVS):
        j = k * 37 % DEVS
        c, yy, zz, xx = rows[j // 64], ys[j // 16 % 4], zs[j // 4 % 4], xs[j % 4]
        o, t = yy * 2 + c, zz * 4 + xx
        pltpu.make_async_remote_copy(
            src.at[part_of(o, t)],
            dst.at[me],
            send_sem,
            recv_sem,
            device_id=(o, t),
            device_id_type=MESH,
        ).start()


def iota(shape, dim):
    return lax.broadcasted_iota(jnp.int32, shape, dim)


def column(row):
    return jnp.broadcast_to(row, (128, row.shape[1])).T


def kernel(
    x_ref,
    pos_ref,
    bc_ref,
    out_ref,
    unit,
    posc,
    send,
    recv,
    parts,
    bc_here,
    bc_got,
    pos_row,
    clr,
    clc,
    acc,
    acc_got,
    small_send,
    small_got,
    ret_got,
    rank_ref,
    send_sem,
    recv_sem,
    bc_sem,
    copy_send,
    copy_recv,
    cl_send,
    cl_recv,
    acc_send,
    acc_recv,
    ret_sems,
    local_sem,
    entry_sem,
    meta_sems,
):
    owner, tile = lax.axis_index("owner"), lax.axis_index("tile")
    me = part_of(owner, tile)
    core = owner % 2
    y, z, x = owner // 2, tile // 4, tile % 4
    q = me % 4
    base = me - me % 16
    barrier = pltpu.get_barrier_semaphore()

    for k in range(1, 16):
        pl.semaphore_signal(
            barrier, inc=1, device_id=(owner, (tile + k) % 16), device_id_type=MESH
        )
    for k in range(1, 8):
        pl.semaphore_signal(barrier, inc=1, device_id=((owner + k) % 8, tile), device_id_type=MESH)

    pos = pos_ref[...]
    posf = pos.astype(F32)
    posc[...] = column(posf)
    for t in range(ROWS // 128):
        here = posf[:, t * 128 : (t + 1) * 128]
        less = jnp.where(posc[...] < here, 1.0, 0.0)
        rank_ref[:, t * 128 : (t + 1) * 128] = jnp.sum(less, axis=0, keepdims=True).astype(jnp.int32)

    @pl.loop(0, ROWS // 128)
    def _(c):
        rows = pl.ds(pl.multiple_of(c * 128, 128), 128)
        v = x_ref[rows, :].astype(F32)
        s = lax.rsqrt(jnp.sum(v * v, axis=1, keepdims=True) + 1e-06)
        unit[rows, :] = (v * s).astype(BF16)

    @pl.loop(0, CHUNKS)
    def _(c):
        pick = jnp.where(rank_ref[...] == iota((CHUNK, ROWS), 0) + c * CHUNK, 1.0, 0.0).astype(BF16)
        got = jnp.dot(pick, unit[...], preferred_element_type=F32)
        blocks = CHUNK // PAIR
        send[pl.ds(c * blocks, blocks)] = got.reshape(blocks, PAIR, D).astype(BF16)

    rank = rank_ref[...]
    inside = (pos % ROWS).astype(F32)
    group = jnp.where(rank // PAIR == iota((DEVS, ROWS), 0), inside, 0.0)
    turn = jnp.where(rank % PAIR == iota((128, ROWS), 0), 1.0, 0.0)
    meta = lax.dot_general(group, turn, NT, precision=HIGH, preferred_element_type=F32)
    small_send[0] = meta.reshape(DEVS, 1, 128)

    for b in range(ROWS // BLK):
        bc_here[b : b + 1, :] = jnp.full((1, 128), bc_ref[b], jnp.int32).astype(F32)

    pl.semaphore_wait(barrier, 22)
    for k in range(1, 8):
        pl.semaphore_signal(entry_sem, inc=1, device_id=((owner + k) % 8, tile), device_id_type=MESH)
    pl.semaphore_wait(entry_sem, 7)

    listed = owner * 16 + tile

    @pl.when(listed != me)
    def _():
        pltpu.make_async_remote_copy(
            bc_here, bc_got, bc_sem.at[0], bc_sem.at[1], device_id=place(listed), device_id_type=MESH
        ).start()

    @pl.when(listed == me)
    def _():
        pltpu.make_async_copy(bc_here, bc_got, bc_sem.at[1]).start()

    own = pltpu.make_async_copy(send.at[me], recv.at[me], local_sem.at[0])
    own.start()
    own_meta = pltpu.make_async_copy(small_send.at[0, me], small_got.at[me], local_sem.at[1])
    own_meta.start()
    all_to_all(send, recv, me, core, y, z, x, send_sem, recv_sem)
    all_to_all(small_send.at[0], small_got, me, core, y, z, x, meta_sems.at[0], meta_sems.at[1])
    most = pl.ds(0, DEVS - 1)
    own.wait()
    pltpu.make_async_copy(send.at[most], recv.at[most], recv_sem).wait()

    step = jnp.where(core == 0, 1, 3)
    back = base + ((x + 4 - step) % 4) * 4 + q
    back2 = base + ((x + 2) % 4) * 4 + q
    ahead = base + ((x + step) % 4) * 4 + q
    flip_y = me - q + (q + 2) % 4
    flip_z = me - q + (q // 2) * 2 + (q + 1) % 2
    flip_yz = me - q + 3 - q

    def part_copy(src, c, dst, to):
        rows = pl.ds(c * CHUNK, CHUNK)
        return pltpu.make_async_remote_copy(
            parts.at[src, rows],
            parts.at[dst, rows],
            copy_send.at[dst, c],
            copy_recv.at[dst, c],
            device_id=place(to),
            device_id_type=MESH,
        )

    def arrived(slot, c):
        rows = pl.ds(c * CHUNK, CHUNK)
        pltpu.make_async_copy(parts.at[slot, rows], parts.at[slot, rows], copy_recv.at[slot, c]).wait()

    def ready(c):
        rows = pl.ds(c * CHUNK, CHUNK)
        blocks = CHUNK // PAIR
        parts[0, rows, :] = recv[pl.ds(c * blocks, blocks)].astype(F32).reshape(CHUNK, D).astype(BF16)
        for dst, to in ((1, back), (3, flip_y), (4, flip_z)):
            part_copy(0, c, dst, to).start()

    ready(0)
    own_meta.wait()
    pltpu.make_async_copy(small_send.at[0, most], small_got.at[most], meta_sems.at[1]).wait()
    pltpu.make_async_copy(bc_here, bc_got, bc_sem.at[1]).wait()

    @pl.when(listed != me)
    def _():
        pltpu.make_async_copy(bc_here, bc_got, bc_sem.at[0]).wait()

    got = small_got[...].reshape(DEVS, 128)
    turn = jnp.where(iota((128, ROWS), 1) % PAIR == iota((128, ROWS), 0), 1.0, 0.0)
    at_row = jnp.dot(got, turn, precision=HIGH, preferred_element_type=F32)
    at_row = jnp.where(iota((DEVS, ROWS), 1) // PAIR == iota((DEVS, ROWS), 0), at_row, 0.0)
    own_pos = jnp.sum(at_row, axis=0, keepdims=True)
    pos_row[...] = jnp.broadcast_to(own_pos, (8, ROWS))
    block = own_pos.astype(jnp.int32) // BLK
    own_cl = jnp.zeros((1, ROWS), F32)
    for b in range(ROWS // BLK):
        own_cl = own_cl + jnp.where(block == b, bc_got[b : b + 1, 0:1], 0.0)
    clr[0] = jnp.broadcast_to(own_cl, (8, ROWS))
    for dst, to in ((1, back), (2, back2), (3, flip_y), (4, flip_z), (5, flip_yz)):
        pltpu.make_async_remote_copy(
            clr.at[0], clr.at[dst], cl_send.at[dst], cl_recv.at[dst], device_id=place(to), device_id_type=MESH
        ).start()
    for c in range(1, CHUNKS):
        ready(c)
    clc[0] = column(own_cl)
    posc[...] = column(pos_row[0:1])
    for m in range(SLOTS):
        acc[m] = jnp.full((8, ROWS), -1.0, F32)

    def fold(s, mask, hi, cols):
        kept = jnp.where(mask, s, -1.0)
        top = jnp.max(kept.reshape(kept.shape[0] // 8, 8, kept.shape[1]), axis=0)
        acc[hi, :, cols] = jnp.maximum(acc[hi, :, cols], top)

    def block_pair(lo, row, m, hi, col, n, diag=False):
        rows = pl.ds(pl.multiple_of(row, m), m)
        cols = pl.ds(pl.multiple_of(col, n), n)
        s = lax.dot_general(parts[lo, rows, :], parts[hi, cols, :], NT, preferred_element_type=F32)
        for k in range(n // 128):
            at = pl.ds(pl.multiple_of(col + k * 128, 128), 128)
            mask = clc[lo, rows, :] == clr[hi, 0:1, at]
            if diag:
                mask = mask & (posc[rows, :] < pos_row[0:1, at])
            fold(s[:, k * 128 : (k + 1) * 128], mask, hi, at)

    def cl_arrived(slot):
        pltpu.make_async_copy(clr.at[slot], clr.at[slot], cl_recv.at[slot]).wait()
        clc[slot] = column(clr[slot, 0:1])

    low = x < 2

    def forward(c):
        arrived(1, c)
        if c < CHUNKS // 2:

            @pl.when((x + 4 - step) % 4 < 2)
            def _():
                part_copy(1, c, 2, back).start()
        else:
            part_copy(1, c, 2, back).start()
        arrived(3, c)
        if c < CHUNKS // 2:
            part_copy(3, c, 5, flip_z).start()
        arrived(4, c)
        if c >= CHUNKS // 2:
            part_copy(4, c, 5, flip_y).start()

    forward(0)

    @pl.loop(0, 2)
    def _(i):
        block_pair(0, 0, ROWS, 0, i * 512, 512, diag=True)

    forward(1)
    for slot in (1, 3, 4):
        cl_arrived(slot)
    forward(2)
    for slot in (5, 2):
        cl_arrived(slot)
    forward(3)

    ahead_hi = (x + step) % 4 > x

    def with_ahead(face):
        lo = jnp.where(ahead_hi, face, 1)
        hi = jnp.where(ahead_hi, 1, face)

        @pl.loop(0, 2)
        def _(i):
            block_pair(lo, 0, ROWS, hi, i * 512, 512)

    def with_own(slot, mine_lo):
        lo = jnp.where(mine_lo, 0, slot)
        hi = jnp.where(mine_lo, slot, 0)
        block_pair(lo, jnp.where(mine_lo, 0, 512), 512, hi, 0, ROWS)

    with_ahead(0)
    with_ahead(3)
    with_ahead(4)
    with_own(3, flip_y > me)
    with_own(4, flip_z > me)
    for c in range(CHUNKS):
        arrived(5, c)
    with_ahead(5)
    with_own(5, flip_yz > me)

    for n in range(CHUNKS):
        if n < CHUNKS // 2:

            @pl.when(low)
            def _():
                arrived(2, n)

        else:
            arrived(2, n)

        @pl.when(low)
        def _():
            for face in (0, 3, 4, 5):
                block_pair(face, 0, 512, 2, n * CHUNK, CHUNK)

    @pl.when(jnp.logical_not(low))
    def _():
        for face in (0, 3, 4, 5):
            block_pair(2, 512, 512, face, 0, ROWS)

    for dst, to in ((1, ahead), (2, back2), (3, flip_y), (4, flip_z), (5, flip_yz)):
        pltpu.make_async_remote_copy(
            acc.at[dst],
            acc_got.at[dst - 1],
            acc_send.at[dst],
            acc_recv.at[dst],
            device_id=place(to),
            device_id_type=MESH,
        ).start()
    best = acc[0]
    for m in range(1, SLOTS):
        pltpu.make_async_copy(acc_got.at[m - 1], acc_got.at[m - 1], acc_recv.at[m]).wait()
        best = jnp.maximum(best, acc_got[m - 1])
    best = jnp.max(best, axis=0, keepdims=True)

    spread = jnp.where(iota((DEVS, ROWS), 1) // PAIR == iota((DEVS, ROWS), 0), best, 0.0)
    fold8 = jnp.where(iota((ROWS, 128), 0) % PAIR == iota((ROWS, 128), 1), 1.0, 0.0)
    ret = jnp.dot(spread, fold8, precision=HIGH, preferred_element_type=F32)
    small_send[1] = ret.reshape(DEVS, 1, 128)
    back_own = pltpu.make_async_copy(small_send.at[1, me], ret_got.at[me], local_sem.at[0])
    back_own.start()

    all_to_all(small_send.at[1], ret_got, me, core, y, z, x, ret_sems.at[0], ret_sems.at[1])
    back_own.wait()
    pltpu.make_async_copy(small_send.at[1, most], ret_got.at[most], ret_sems.at[1]).wait()
    got = ret_got[...].reshape(DEVS, 128)
    rank = rank_ref[...]
    turn = jnp.where(rank % PAIR == iota((128, ROWS), 0), 1.0, 0.0)
    rows = jnp.dot(got, turn, precision=HIGH, preferred_element_type=F32)
    out_ref[...] = jnp.sum(
        jnp.where(rank // PAIR == iota((DEVS, ROWS), 0), rows, 0.0), axis=0, keepdims=True
    )

    pltpu.make_async_copy(send.at[most], recv.at[most], send_sem).wait()
    pltpu.make_async_copy(small_send.at[0, most], small_got.at[most], meta_sems.at[0]).wait()
    pltpu.make_async_copy(small_send.at[1, most], ret_got.at[most], ret_sems.at[0]).wait()
    for c in range(CHUNKS):
        rows = pl.ds(c * CHUNK, CHUNK)
        for dst in (1, 3, 4, 5):
            pltpu.make_async_copy(parts.at[0, rows], parts.at[dst, rows], copy_send.at[dst, c]).wait()

        @pl.when(((x + 4 - step) % 4 < 2) | (c >= CHUNKS // 2))
        def _():
            pltpu.make_async_copy(parts.at[1, rows], parts.at[2, rows], copy_send.at[2, c]).wait()

    for dst in range(1, SLOTS):
        pltpu.make_async_copy(clr.at[0], clr.at[dst], cl_send.at[dst]).wait()
        pltpu.make_async_copy(acc.at[dst], acc_got.at[dst - 1], acc_send.at[dst]).wait()


def per_device(embeddings, sorted_pos, block_cluster, tile_list):
    del tile_list
    vmem = pl.BlockSpec(memory_space=pltpu.VMEM)
    out = pl.pallas_call(
        kernel,
        out_shape=jax.ShapeDtypeStruct((1, ROWS), F32),
        in_specs=[vmem, vmem, pl.BlockSpec(memory_space=pltpu.SMEM)],
        out_specs=vmem,
        scratch_shapes=[
            pltpu.VMEM((ROWS, D), BF16),
            pltpu.VMEM((ROWS, 128), F32),
            pltpu.VMEM((DEVS, PAIR, D), BF16),
            pltpu.VMEM((DEVS, PAIR, D), BF16),
            pltpu.VMEM((SLOTS, ROWS, D), BF16),
            pltpu.VMEM((8, 128), F32),
            pltpu.VMEM((8, 128), F32),
            pltpu.VMEM((8, ROWS), F32),
            pltpu.VMEM((SLOTS, 8, ROWS), F32),
            pltpu.VMEM((SLOTS, ROWS, 128), F32),
            pltpu.VMEM((SLOTS, 8, ROWS), F32),
            pltpu.VMEM((SLOTS - 1, 8, ROWS), F32),
            pltpu.VMEM((2, DEVS, 1, 128), F32),
            pltpu.VMEM((DEVS, 1, 128), F32),
            pltpu.VMEM((DEVS, 1, 128), F32),
            pltpu.VMEM((1, ROWS), jnp.int32),
            pltpu.SemaphoreType.DMA,
            pltpu.SemaphoreType.DMA,
            pltpu.SemaphoreType.DMA((2,)),
            pltpu.SemaphoreType.DMA((SLOTS, CHUNKS)),
            pltpu.SemaphoreType.DMA((SLOTS, CHUNKS)),
            pltpu.SemaphoreType.DMA((SLOTS,)),
            pltpu.SemaphoreType.DMA((SLOTS,)),
            pltpu.SemaphoreType.DMA((SLOTS,)),
            pltpu.SemaphoreType.DMA((SLOTS,)),
            pltpu.SemaphoreType.DMA((2,)),
            pltpu.SemaphoreType.DMA((2,)),
            pltpu.SemaphoreType.REGULAR,
            pltpu.SemaphoreType.DMA((2,)),
        ],
        compiler_params=pltpu.CompilerParams(
            collective_id=0, has_side_effects=True, vmem_limit_bytes=56 * 1024 * 1024
        ),
    )(embeddings, sorted_pos.reshape(1, ROWS), block_cluster)
    return out.reshape(ROWS)


def solution(mesh):
    placed = (
        P(("owner", "tile"), None),
        P(("owner", "tile")),
        P(("owner", "tile")),
        P("owner", "tile", None, None),
    )
    return jax.shard_map(
        per_device, mesh=mesh, in_specs=placed, out_specs=P(("owner", "tile")), check_vma=False
    )
```

```python
import jax
import jax.numpy as jnp
from jax import lax
from jax.experimental import pallas as pl
from jax.experimental.pallas import tpu as pltpu
from jax.sharding import PartitionSpec as P

D = 1024
BLK = 128
ROWS = 1024
DEVS = 128
PAIR = ROWS // DEVS
CHUNK = 256
CHUNKS = ROWS // CHUNK
SLOTS = 6
F32 = jnp.float32
BF16 = jnp.bfloat16
MESH = pl.DeviceIdType.MESH
NT = (((1,), (1,)), ((), ()))


def place(part):
    core = part // 64
    y = (2 * ((part // 32) % 2) + (part // 2) % 2 + core) % 4
    z = (2 * ((part // 16) % 2) + part % 2 + core) % 4
    x = (part // 4) % 4
    return y * 2 + core, z * 4 + x


def part_of(owner, tile):
    core = owner % 2
    y = (owner // 2 + 4 - core) % 4
    z = (tile // 4 + 4 - core) % 4
    x = tile % 4
    return core * 64 + (y // 2) * 32 + (z // 2) * 16 + x * 4 + (y % 2) * 2 + z % 2


def iota(shape, dim):
    return lax.broadcasted_iota(jnp.int32, shape, dim)


def rows_then_columns(sent, mid, got, owner, tile, sems, local):
    def first():
        stay = pltpu.make_async_copy(sent.at[owner], mid.at[owner], local.at[0])
        stay.start()
        for k in range(1, 8):
            to = (owner + k) % 8
            pltpu.make_async_remote_copy(
                sent.at[to],
                mid.at[owner],
                sems.at[0],
                sems.at[1],
                device_id=(to, tile),
                device_id_type=MESH,
            ).start()

    def second():
        seven = pl.ds(0, 7)
        pltpu.make_async_copy(sent.at[owner], mid.at[owner], local.at[0]).wait()
        pltpu.make_async_copy(sent.at[seven], mid.at[seven], sems.at[1]).wait()
        stay = pltpu.make_async_copy(mid.at[:, tile], got.at[tile], local.at[1])
        stay.start()
        for k in range(1, 16):
            to = (tile + k) % 16
            pltpu.make_async_remote_copy(
                mid.at[:, to],
                got.at[tile],
                sems.at[2],
                sems.at[3],
                device_id=(owner, to),
                device_id_type=MESH,
            ).start()

    def arrive():
        fifteen = pl.ds(0, 15)
        pltpu.make_async_copy(got.at[tile], got.at[tile], local.at[1]).wait()
        pltpu.make_async_copy(got.at[fifteen], got.at[fifteen], sems.at[3]).wait()

    def left():
        seven, fifteen = pl.ds(0, 7), pl.ds(0, 15)
        pltpu.make_async_copy(sent.at[seven], mid.at[seven], sems.at[0]).wait()
        pltpu.make_async_copy(got.at[fifteen], got.at[fifteen], sems.at[2]).wait()

    return first, second, arrive, left


def column(row):
    return jnp.broadcast_to(row, (128, row.shape[1])).T


def kernel(
    x_ref,
    pos_ref,
    bc_ref,
    out_ref,
    unit,
    posc,
    send,
    recv,
    parts,
    bc_here,
    bc_got,
    pos_row,
    clr,
    clc,
    acc,
    acc_got,
    meta_send,
    meta_mid,
    meta_got,
    ret_send,
    ret_got,
    rank_ref,
    turn_ref,
    mine_ref,
    send_sem,
    recv_sem,
    bc_sem,
    copy_send,
    copy_recv,
    cl_send,
    cl_recv,
    acc_send,
    acc_recv,
    ret_sems,
    meta_sems,
    local_sem,
    ret_local,
    meta_local,
):
    owner, tile = lax.axis_index("owner"), lax.axis_index("tile")
    me = part_of(owner, tile)
    core = owner % 2
    y, z, x = owner // 2, tile // 4, tile % 4
    q = me % 4
    base = me - me % 16
    barrier = pltpu.get_barrier_semaphore()

    for k in range(1, DEVS):
        to = ((owner + k // 16) % 8, (tile + k % 16) % 16)
        pl.semaphore_signal(barrier, inc=1, device_id=to, device_id_type=MESH)

    pos = pos_ref[...]
    posf = pos.astype(F32)
    posc[...] = column(posf)
    ranks = []
    for t in range(ROWS // 128):
        here = posf[:, t * 128 : (t + 1) * 128]
        less = jnp.where(posc[...] < here, 1.0, 0.0)
        ranks.append(jnp.sum(less, axis=0, keepdims=True).astype(jnp.int32))
    within = jnp.concatenate(ranks, axis=1) & (PAIR - 1)
    to_o, to_t = place(pos >> 10)
    rank_ref[...] = (to_o * 16 + to_t) * PAIR + within

    @pl.loop(0, ROWS // 128)
    def _(c):
        rows = pl.ds(pl.multiple_of(c * 128, 128), 128)
        v = x_ref[rows, :].astype(F32)
        s = lax.rsqrt(jnp.sum(v * v, axis=1, keepdims=True) + 1e-06)
        unit[rows, :] = (v * s).astype(BF16)

    @pl.loop(0, CHUNKS)
    def _(c):
        pick = jnp.where(rank_ref[...] == iota((CHUNK, ROWS), 0) + c * CHUNK, 1.0, 0.0).astype(BF16)
        got = jnp.dot(pick, unit[...], preferred_element_type=F32)
        blocks = CHUNK // PAIR
        send[pl.ds(c * blocks, blocks)] = got.reshape(blocks, PAIR, D).astype(BF16)

    inside = pos & (ROWS - 1)
    here = iota((DEVS, ROWS), 0) == to_o * 16 + to_t
    high = jnp.where(here, (inside >> 5).astype(F32), 0.0).astype(BF16)
    below = jnp.where(here, (inside & 31).astype(F32), 0.0).astype(BF16)
    lane = iota((128, ROWS), 0)
    turn = jnp.where(lane == within, 1.0, 0.0).astype(BF16)
    turn2 = jnp.where(lane == within + PAIR, 1.0, 0.0).astype(BF16)
    meta = lax.dot_general(high, turn, NT, preferred_element_type=F32)
    meta = meta + lax.dot_general(below, turn2, NT, preferred_element_type=F32)
    meta_send[...] = meta.reshape(8, 16, 1, 128)
    turn_ref[...] = turn
    mine_ref[...] = jnp.where(here, 1.0, 0.0)

    for b in range(ROWS // BLK):
        bc_here[b : b + 1, :] = jnp.full((1, 128), bc_ref[b], jnp.int32).astype(F32)

    pl.semaphore_wait(barrier, DEVS - 1)

    listed = owner * 16 + tile

    @pl.when(listed != me)
    def _():
        pltpu.make_async_remote_copy(
            bc_here, bc_got, bc_sem.at[0], bc_sem.at[1], device_id=place(listed), device_id_type=MESH
        ).start()

    @pl.when(listed == me)
    def _():
        pltpu.make_async_copy(bc_here, bc_got, bc_sem.at[1]).start()

    meta_first, meta_second, meta_arrive, meta_left = rows_then_columns(
        meta_send, meta_mid, meta_got, owner, tile, meta_sems, meta_local
    )
    meta_first()

    dev = owner * 16 + tile
    own = pltpu.make_async_copy(send.at[dev], recv.at[dev], local_sem)
    own.start()

    def send_rows(first, last):
        @pl.loop(first, last)
        def _(k):
            j = k * 37 % DEVS
            o = (owner + j // 16) % 8
            t = (tile // 4 + j // 4) % 4 * 4 + (tile + j) % 4
            pltpu.make_async_remote_copy(
                send.at[o * 16 + t],
                recv.at[dev],
                send_sem,
                recv_sem,
                device_id=(o, t),
                device_id_type=MESH,
            ).start()

    send_rows(1, 48)
    meta_second()
    send_rows(48, DEVS)

    meta_arrive()
    pltpu.make_async_copy(bc_here, bc_got, bc_sem.at[1]).wait()

    @pl.when(listed != me)
    def _():
        pltpu.make_async_copy(bc_here, bc_got, bc_sem.at[0]).wait()

    got = meta_got[...].reshape(DEVS, 128).astype(BF16)
    lane, at = iota((128, ROWS), 0), iota((128, ROWS), 1)
    turn = jnp.where(lane == (at & 7), 32.0, jnp.where(lane == (at & 7) + PAIR, 1.0, 0.0)).astype(BF16)
    at_row = jnp.dot(got, turn, preferred_element_type=F32)
    source = iota((DEVS, ROWS), 1) >> 3
    at_row = jnp.where((source & 15) * 8 + (source >> 4) == iota((DEVS, ROWS), 0), at_row, 0.0)
    own_pos = jnp.sum(at_row, axis=0, keepdims=True)
    pos_row[...] = jnp.broadcast_to(own_pos, (8, ROWS))
    block = own_pos.astype(jnp.int32) >> 7
    own_cl = jnp.zeros((1, ROWS), F32)
    for b in range(ROWS // BLK):
        own_cl = own_cl + jnp.where(block == b, bc_got[b : b + 1, 0:1], 0.0)
    clr[0] = jnp.broadcast_to(own_cl, (8, ROWS))
    step = jnp.where(core == 0, 1, 3)
    back = base + ((x + 4 - step) % 4) * 4 + q
    back2 = base + ((x + 2) % 4) * 4 + q
    ahead = base + ((x + step) % 4) * 4 + q
    flip_y = me - q + (q + 2) % 4
    flip_z = me - q + (q // 2) * 2 + (q + 1) % 2
    flip_yz = me - q + 3 - q

    for dst, to in ((1, back), (2, back2), (3, flip_y), (4, flip_z), (5, flip_yz)):
        pltpu.make_async_remote_copy(
            clr.at[0], clr.at[dst], cl_send.at[dst], cl_recv.at[dst], device_id=place(to), device_id_type=MESH
        ).start()
    clc[0] = column(own_cl)
    posc[...] = column(own_pos)
    for m in range(SLOTS):
        acc[m] = jnp.full((8, ROWS), -1.0, F32)

    most = pl.ds(0, DEVS - 1)
    own.wait()
    pltpu.make_async_copy(send.at[most], recv.at[most], recv_sem).wait()

    def part_copy(src, c, dst, to):
        rows = pl.ds(c * CHUNK, CHUNK)
        return pltpu.make_async_remote_copy(
            parts.at[src, rows],
            parts.at[dst, rows],
            copy_send.at[dst, c],
            copy_recv.at[dst, c],
            device_id=place(to),
            device_id_type=MESH,
        )

    def arrived(slot, c):
        rows = pl.ds(c * CHUNK, CHUNK)
        pltpu.make_async_copy(parts.at[slot, rows], parts.at[slot, rows], copy_recv.at[slot, c]).wait()

    def ready(c):
        rows = pl.ds(c * CHUNK, CHUNK)
        blocks = CHUNK // PAIR
        parts[0, rows, :] = recv[pl.ds(c * blocks, blocks)].astype(F32).reshape(CHUNK, D).astype(BF16)
        for dst, to in ((1, back), (3, flip_y), (4, flip_z)):
            part_copy(0, c, dst, to).start()

    for c in range(CHUNKS):
        ready(c)

    def fold(s, mask, hi, cols):
        kept = jnp.where(mask, s, -1.0)
        top = jnp.max(kept.reshape(kept.shape[0] // 8, 8, kept.shape[1]), axis=0)
        acc[hi, :, cols] = jnp.maximum(acc[hi, :, cols], top)

    def block_pair(lo, row, m, hi, col, n, diag=False):
        rows = pl.ds(pl.multiple_of(row, m), m)
        cols = pl.ds(pl.multiple_of(col, n), n)
        s = lax.dot_general(parts[lo, rows, :], parts[hi, cols, :], NT, preferred_element_type=F32)
        for k in range(n // 128):
            at = pl.ds(pl.multiple_of(col + k * 128, 128), 128)
            mask = clc[lo, rows, :] == clr[hi, 0:1, at]
            if diag:
                mask = mask & (posc[rows, :] < pos_row[0:1, at])
            fold(s[:, k * 128 : (k + 1) * 128], mask, hi, at)

    low = x < 2

    def forward(c):
        arrived(1, c)
        if c < CHUNKS // 2:

            @pl.when((x + 4 - step) % 4 < 2)
            def _():
                part_copy(1, c, 2, back).start()
        else:
            part_copy(1, c, 2, back).start()
        arrived(3, c)
        if c < CHUNKS // 2:
            part_copy(3, c, 5, flip_z).start()
        arrived(4, c)
        if c >= CHUNKS // 2:
            part_copy(4, c, 5, flip_y).start()

    forward(0)

    @pl.loop(0, 2)
    def _(i):
        block_pair(0, 0, ROWS, 0, i * 512, 512, diag=True)

    forward(1)
    for slot in range(1, SLOTS):
        pltpu.make_async_copy(clr.at[slot], clr.at[slot], cl_recv.at[slot]).wait()
        clc[slot] = column(clr[slot, 0:1])

    forward(2)
    forward(3)

    ahead_hi = (x + step) % 4 > x

    def with_ahead(face):
        lo = jnp.where(ahead_hi, face, 1)
        hi = jnp.where(ahead_hi, 1, face)

        @pl.loop(0, 2)
        def _(i):
            block_pair(lo, 0, ROWS, hi, i * 512, 512)

    def with_own(slot, mine_lo):
        lo = jnp.where(mine_lo, 0, slot)
        hi = jnp.where(mine_lo, slot, 0)
        block_pair(lo, jnp.where(mine_lo, 0, 512), 512, hi, 0, ROWS)

    with_ahead(0)
    with_ahead(3)
    with_ahead(4)
    with_own(3, flip_y > me)
    with_own(4, flip_z > me)
    for c in range(CHUNKS):
        arrived(5, c)
    with_ahead(5)
    with_own(5, flip_yz > me)

    for n in range(CHUNKS):
        if n < CHUNKS // 2:

            @pl.when(low)
            def _():
                arrived(2, n)

        else:
            arrived(2, n)

        @pl.when(low)
        def _():
            for face in (0, 3, 4, 5):
                block_pair(face, 0, 512, 2, n * CHUNK, CHUNK)

    @pl.when(jnp.logical_not(low))
    def _():
        for face in (0, 3, 4, 5):
            block_pair(2, 512, 512, face, 0, ROWS)

    for dst, to in ((1, ahead), (2, back2), (3, flip_y), (4, flip_z), (5, flip_yz)):
        pltpu.make_async_remote_copy(
            acc.at[dst],
            acc_got.at[dst - 1],
            acc_send.at[dst],
            acc_recv.at[dst],
            device_id=place(to),
            device_id_type=MESH,
        ).start()
    best = acc[0]
    for m in range(1, SLOTS):
        pltpu.make_async_copy(acc_got.at[m - 1], acc_got.at[m - 1], acc_recv.at[m]).wait()
        best = jnp.maximum(best, acc_got[m - 1])
    best = jnp.max(best, axis=0, keepdims=True)

    each = column(best).reshape(DEVS, PAIR, 128)
    each = jnp.where(iota((DEVS, PAIR, 128), 1) == iota((DEVS, PAIR, 128), 2), each, 0.0)
    ret_send[...] = jnp.sum(each, axis=1, keepdims=True)
    stay = pltpu.make_async_copy(ret_send.at[dev], ret_got.at[dev], ret_local)
    stay.start()
    for k in range(1, DEVS):
        j = k * 37 % DEVS
        o, t = (owner + j // 16) % 8, (tile + j % 16) % 16
        pltpu.make_async_remote_copy(
            ret_send.at[o * 16 + t],
            ret_got.at[dev],
            ret_sems.at[0],
            ret_sems.at[1],
            device_id=(o, t),
            device_id_type=MESH,
        ).start()
    stay.wait()
    pltpu.make_async_copy(ret_send.at[most], ret_got.at[most], ret_sems.at[1]).wait()
    got = ret_got[...].reshape(DEVS, 128)
    one = got.astype(BF16)
    rest = got - one.astype(F32)
    two = rest.astype(BF16)
    three = (rest - two.astype(F32)).astype(BF16)
    turn = turn_ref[...]
    rows = jnp.dot(one, turn, preferred_element_type=F32)
    rows = rows + jnp.dot(two, turn, preferred_element_type=F32)
    rows = rows + jnp.dot(three, turn, preferred_element_type=F32)
    out_ref[...] = jnp.sum(rows * mine_ref[...], axis=0, keepdims=True)

    pltpu.make_async_copy(send.at[most], recv.at[most], send_sem).wait()
    meta_left()
    pltpu.make_async_copy(ret_send.at[most], ret_got.at[most], ret_sems.at[0]).wait()
    for c in range(CHUNKS):
        rows = pl.ds(c * CHUNK, CHUNK)
        for dst in (1, 3, 4, 5):
            pltpu.make_async_copy(parts.at[0, rows], parts.at[dst, rows], copy_send.at[dst, c]).wait()

        @pl.when(((x + 4 - step) % 4 < 2) | (c >= CHUNKS // 2))
        def _():
            pltpu.make_async_copy(parts.at[1, rows], parts.at[2, rows], copy_send.at[2, c]).wait()

    for dst in range(1, SLOTS):
        pltpu.make_async_copy(clr.at[0], clr.at[dst], cl_send.at[dst]).wait()
        pltpu.make_async_copy(acc.at[dst], acc_got.at[dst - 1], acc_send.at[dst]).wait()


def per_device(embeddings, sorted_pos, block_cluster, tile_list):
    del tile_list
    vmem = pl.BlockSpec(memory_space=pltpu.VMEM)
    out = pl.pallas_call(
        kernel,
        out_shape=jax.ShapeDtypeStruct((1, ROWS), F32),
        in_specs=[vmem, vmem, pl.BlockSpec(memory_space=pltpu.SMEM)],
        out_specs=vmem,
        scratch_shapes=[
            pltpu.VMEM((ROWS, D), BF16),
            pltpu.VMEM((ROWS, 128), F32),
            pltpu.VMEM((DEVS, PAIR, D), BF16),
            pltpu.VMEM((DEVS, PAIR, D), BF16),
            pltpu.VMEM((SLOTS, ROWS, D), BF16),
            pltpu.VMEM((8, 128), F32),
            pltpu.VMEM((8, 128), F32),
            pltpu.VMEM((8, ROWS), F32),
            pltpu.VMEM((SLOTS, 8, ROWS), F32),
            pltpu.VMEM((SLOTS, ROWS, 128), F32),
            pltpu.VMEM((SLOTS, 8, ROWS), F32),
            pltpu.VMEM((SLOTS - 1, 8, ROWS), F32),
            pltpu.VMEM((8, 16, 1, 128), F32),
            pltpu.VMEM((8, 16, 1, 128), F32),
            pltpu.VMEM((16, 8, 1, 128), F32),
            pltpu.VMEM((DEVS, 1, 128), F32),
            pltpu.VMEM((DEVS, 1, 128), F32),
            pltpu.VMEM((1, ROWS), jnp.int32),
            pltpu.VMEM((128, ROWS), BF16),
            pltpu.VMEM((DEVS, ROWS), F32),
            pltpu.SemaphoreType.DMA,
            pltpu.SemaphoreType.DMA,
            pltpu.SemaphoreType.DMA((2,)),
            pltpu.SemaphoreType.DMA((SLOTS, CHUNKS)),
            pltpu.SemaphoreType.DMA((SLOTS, CHUNKS)),
            pltpu.SemaphoreType.DMA((SLOTS,)),
            pltpu.SemaphoreType.DMA((SLOTS,)),
            pltpu.SemaphoreType.DMA((SLOTS,)),
            pltpu.SemaphoreType.DMA((SLOTS,)),
            pltpu.SemaphoreType.DMA((2,)),
            pltpu.SemaphoreType.DMA((4,)),
            pltpu.SemaphoreType.DMA,
            pltpu.SemaphoreType.DMA,
            pltpu.SemaphoreType.DMA((2,)),
        ],
        compiler_params=pltpu.CompilerParams(
            collective_id=0, has_side_effects=True, vmem_limit_bytes=56 * 1024 * 1024
        ),
    )(embeddings, sorted_pos.reshape(1, ROWS), block_cluster)
    return out.reshape(ROWS)


def solution(mesh):
    placed = (
        P(("owner", "tile"), None),
        P(("owner", "tile")),
        P(("owner", "tile")),
        P("owner", "tile", None, None),
    )
    return jax.shard_map(
        per_device, mesh=mesh, in_specs=placed, out_specs=P(("owner", "tile")), check_vma=False
    )
```

```python
import jax
import jax.numpy as jnp
from jax import lax
from jax.experimental import pallas as pl
from jax.experimental.pallas import tpu as pltpu
from jax.sharding import PartitionSpec as P

D = 1024
BLK = 128
ROWS = 1024
DEVS = 128
PAIR = ROWS // DEVS
CHUNK = 256
CHUNKS = ROWS // CHUNK
SLOTS = 6
F32 = jnp.float32
BF16 = jnp.bfloat16
MESH = pl.DeviceIdType.MESH
NT = (((1,), (1,)), ((), ()))


def place(part):
    core = part // 64
    y = (2 * ((part // 32) % 2) + (part // 2) % 2 + core) % 4
    z = (2 * ((part // 16) % 2) + part % 2 + core) % 4
    x = (part // 4) % 4
    return y * 2 + core, z * 4 + x


def part_of(owner, tile):
    core = owner % 2
    y = (owner // 2 + 4 - core) % 4
    z = (tile // 4 + 4 - core) % 4
    x = tile % 4
    return core * 64 + (y // 2) * 32 + (z // 2) * 16 + x * 4 + (y % 2) * 2 + z % 2


def iota(shape, dim):
    return lax.broadcasted_iota(jnp.int32, shape, dim)


def rows_then_columns(sent, mid, got, owner, tile, sems, local):
    def first():
        stay = pltpu.make_async_copy(sent.at[owner], mid.at[owner], local.at[0])
        stay.start()
        for k in range(1, 8):
            to = (owner + k) % 8
            pltpu.make_async_remote_copy(
                sent.at[to],
                mid.at[owner],
                sems.at[0],
                sems.at[1],
                device_id=(to, tile),
                device_id_type=MESH,
            ).start()

    def second():
        seven = pl.ds(0, 7)
        pltpu.make_async_copy(sent.at[owner], mid.at[owner], local.at[0]).wait()
        pltpu.make_async_copy(sent.at[seven], mid.at[seven], sems.at[1]).wait()
        stay = pltpu.make_async_copy(mid.at[:, tile], got.at[tile], local.at[1])
        stay.start()
        for k in range(1, 16):
            to = (tile + k) % 16
            pltpu.make_async_remote_copy(
                mid.at[:, to],
                got.at[tile],
                sems.at[2],
                sems.at[3],
                device_id=(owner, to),
                device_id_type=MESH,
            ).start()

    def arrive():
        fifteen = pl.ds(0, 15)
        pltpu.make_async_copy(got.at[tile], got.at[tile], local.at[1]).wait()
        pltpu.make_async_copy(got.at[fifteen], got.at[fifteen], sems.at[3]).wait()

    def left():
        seven, fifteen = pl.ds(0, 7), pl.ds(0, 15)
        pltpu.make_async_copy(sent.at[seven], mid.at[seven], sems.at[0]).wait()
        pltpu.make_async_copy(got.at[fifteen], got.at[fifteen], sems.at[2]).wait()

    return first, second, arrive, left


def column(row):
    return jnp.broadcast_to(row, (128, row.shape[1])).T


def kernel(
    x_hbm,
    pos_ref,
    bc_ref,
    out_ref,
    x_ref,
    unit,
    posc,
    send,
    recv,
    parts,
    bc_here,
    bc_got,
    pos_row,
    clr,
    clc,
    acc,
    acc_got,
    meta_send,
    meta_mid,
    meta_got,
    ret_send,
    ret_got,
    rank_ref,
    turn_ref,
    mine_ref,
    send_sem,
    rows_sem,
    bc_sem,
    copy_send,
    copy_recv,
    cl_send,
    cl_recv,
    acc_send,
    acc_recv,
    ret_sems,
    meta_sems,
    keep_sem,
    ret_local,
    meta_local,
):
    owner, tile = lax.axis_index("owner"), lax.axis_index("tile")
    me = part_of(owner, tile)
    core = owner % 2
    y, z, x = owner // 2, tile // 4, tile % 4
    q = me % 4
    base = me - me % 16
    barrier = pltpu.get_barrier_semaphore()
    x_in = pltpu.make_async_copy(x_hbm, x_ref, ret_local)
    x_in.start()

    for k in range(1, DEVS):
        to = ((owner + k // 16) % 8, (tile + k % 16) % 16)
        pl.semaphore_signal(barrier, inc=1, device_id=to, device_id_type=MESH)

    pos = pos_ref[...]
    posf = pos.astype(F32)
    posc[...] = column(posf)
    ranks = []
    for t in range(ROWS // 128):
        here = posf[:, t * 128 : (t + 1) * 128]
        less = jnp.where(posc[...] < here, 1.0, 0.0)
        ranks.append(jnp.sum(less, axis=0, keepdims=True).astype(jnp.int32))
    within = jnp.concatenate(ranks, axis=1) & (PAIR - 1)
    to_o, to_t = place(pos >> 10)
    rank_ref[...] = (to_o * 16 + to_t) * PAIR + within

    x_in.wait()

    @pl.loop(0, ROWS // 128)
    def _(c):
        rows = pl.ds(pl.multiple_of(c * 128, 128), 128)
        v = x_ref[rows, :].astype(F32)
        s = lax.rsqrt(jnp.sum(v * v, axis=1, keepdims=True) + 1e-06)
        unit[rows, :] = (v * s).astype(BF16)

    @pl.loop(0, CHUNKS)
    def _(c):
        pick = jnp.where(rank_ref[...] == iota((CHUNK, ROWS), 0) + c * CHUNK, 1.0, 0.0).astype(BF16)
        got = jnp.dot(pick, unit[...], preferred_element_type=F32)
        blocks = CHUNK // PAIR
        send[pl.ds(c * blocks, blocks)] = got.reshape(blocks, PAIR, D).astype(BF16)

    inside = pos & (ROWS - 1)
    here = iota((DEVS, ROWS), 0) == to_o * 16 + to_t
    high = jnp.where(here, (inside >> 5).astype(F32), 0.0).astype(BF16)
    below = jnp.where(here, (inside & 31).astype(F32), 0.0).astype(BF16)
    lane = iota((128, ROWS), 0)
    turn = jnp.where(lane == within, 1.0, 0.0).astype(BF16)
    turn2 = jnp.where(lane == within + PAIR, 1.0, 0.0).astype(BF16)
    meta = lax.dot_general(high, turn, NT, preferred_element_type=F32)
    meta = meta + lax.dot_general(below, turn2, NT, preferred_element_type=F32)
    meta_send[...] = meta.reshape(8, 16, 1, 128)
    turn_ref[...] = turn
    mine_ref[...] = jnp.where(here, 1.0, 0.0)

    for b in range(ROWS // BLK):
        bc_here[b : b + 1, :] = jnp.full((1, 128), bc_ref[b], jnp.int32).astype(F32)

    pl.semaphore_wait(barrier, DEVS - 1)

    listed = owner * 16 + tile

    @pl.when(listed != me)
    def _():
        pltpu.make_async_remote_copy(
            bc_here, bc_got, bc_sem.at[0], bc_sem.at[1], device_id=place(listed), device_id_type=MESH
        ).start()

    @pl.when(listed == me)
    def _():
        pltpu.make_async_copy(bc_here, bc_got, bc_sem.at[1]).start()

    step = jnp.where(core == 0, 1, 3)

    def send_rows(r, block, first):
        @pl.loop(first, 32)
        def _(k):
            j = k * 13 % 32
            o, zz = (owner + j // 4) % 8, (z + j) % 4
            column_of = (x + r * (4 - (1 + 2 * (o % 2)))) % 4
            to_x = column_of if r == 1 else x
            pltpu.make_async_remote_copy(
                send.at[o * 16 + zz * 4 + column_of],
                recv.at[block, owner * 4 + z],
                send_sem,
                rows_sem.at[block],
                device_id=(o, zz * 4 + to_x),
                device_id_type=MESH,
            ).start()

    def keep_rows(r, block):
        column_of = (x + r * (4 - step)) % 4
        return pltpu.make_async_copy(
            send.at[owner * 16 + z * 4 + column_of], recv.at[block, owner * 4 + z], keep_sem.at[block]
        )

    meta_first, meta_second, meta_arrive, meta_left = rows_then_columns(
        meta_send, meta_mid, meta_got, owner, tile, meta_sems, meta_local
    )
    meta_first()
    keep_rows(2, 3).start()
    keep_rows(3, 2).start()
    keep_rows(0, 0).start()
    send_rows(2, 3, 1)
    meta_second()
    send_rows(3, 2, 1)
    send_rows(0, 0, 1)
    send_rows(1, 1, 0)

    back = base + ((x + 4 - step) % 4) * 4 + q
    back2 = base + ((x + 2) % 4) * 4 + q
    ahead = base + ((x + step) % 4) * 4 + q
    flip_y = me - q + (q + 2) % 4
    flip_z = me - q + (q // 2) * 2 + (q + 1) % 2
    flip_yz = me - q + 3 - q

    meta_arrive()
    pltpu.make_async_copy(bc_here, bc_got, bc_sem.at[1]).wait()

    @pl.when(listed != me)
    def _():
        pltpu.make_async_copy(bc_here, bc_got, bc_sem.at[0]).wait()

    got = meta_got[...].reshape(DEVS, 128).astype(BF16)
    lane, at = iota((128, ROWS), 0), iota((128, ROWS), 1)
    turn = jnp.where(lane == (at & 7), 32.0, jnp.where(lane == (at & 7) + PAIR, 1.0, 0.0)).astype(BF16)
    at_row = jnp.dot(got, turn, preferred_element_type=F32)
    source = iota((DEVS, ROWS), 1) >> 3
    source_x = (x + (source >> 5) * step) & 3
    source = ((source & 3) * 4 + source_x) * 8 + ((source >> 2) & 7)
    at_row = jnp.where(source == iota((DEVS, ROWS), 0), at_row, 0.0)
    own_pos = jnp.sum(at_row, axis=0, keepdims=True)
    pos_row[...] = jnp.broadcast_to(own_pos, (8, ROWS))
    block = own_pos.astype(jnp.int32) >> 7
    own_cl = jnp.zeros((1, ROWS), F32)
    for b in range(ROWS // BLK):
        own_cl = own_cl + jnp.where(block == b, bc_got[b : b + 1, 0:1], 0.0)
    clr[0] = jnp.broadcast_to(own_cl, (8, ROWS))
    for dst, to in ((1, back), (2, back2), (3, flip_y), (4, flip_z), (5, flip_yz)):
        pltpu.make_async_remote_copy(
            clr.at[0], clr.at[dst], cl_send.at[dst], cl_recv.at[dst], device_id=place(to), device_id_type=MESH
        ).start()
    clc[0] = column(own_cl)
    posc[...] = column(own_pos)
    for m in range(SLOTS):
        acc[m] = jnp.full((8, ROWS), -1.0, F32)

    def part_copy(src, c, dst, to):
        rows = pl.ds(c * CHUNK, CHUNK)
        return pltpu.make_async_remote_copy(
            parts.at[src, rows],
            parts.at[dst, rows],
            copy_send.at[dst, c],
            copy_recv.at[dst, c],
            device_id=place(to),
            device_id_type=MESH,
        )

    def arrived(slot, c):
        rows = pl.ds(c * CHUNK, CHUNK)
        pltpu.make_async_copy(parts.at[slot, rows], parts.at[slot, rows], copy_recv.at[slot, c]).wait()

    def rows_in(block, slot, r, remote):
        most = pl.ds(0, remote)
        pltpu.make_async_copy(recv.at[block, most], recv.at[block, most], rows_sem.at[block]).wait()
        if remote < 32:
            keep_rows(r, block).wait()
        rows = pl.ds(r * CHUNK, CHUNK)
        parts[slot, rows, :] = recv[block].astype(F32).reshape(CHUNK, D).astype(BF16)

    rows_in(3, 2, 2, 31)
    part_copy(2, 2, 1, ahead).start()
    rows_in(2, 1, 3, 31)
    part_copy(1, 3, 0, ahead).start()
    part_copy(1, 3, 2, back).start()

    def fold(s, mask, hi, cols):
        kept = jnp.where(mask, s, -1.0)
        top = jnp.max(kept.reshape(kept.shape[0] // 8, 8, kept.shape[1]), axis=0)
        acc[hi, :, cols] = jnp.maximum(acc[hi, :, cols], top)

    def block_pair(lo, row, m, hi, col, n, diag=False):
        rows = pl.ds(pl.multiple_of(row, m), m)
        cols = pl.ds(pl.multiple_of(col, n), n)
        s = lax.dot_general(parts[lo, rows, :], parts[hi, cols, :], NT, preferred_element_type=F32)
        for k in range(n // 128):
            at = pl.ds(pl.multiple_of(col + k * 128, 128), 128)
            mask = clc[lo, rows, :] == clr[hi, 0:1, at]
            if diag:
                mask = mask & (posc[rows, :] < pos_row[0:1, at])
            fold(s[:, k * 128 : (k + 1) * 128], mask, hi, at)

    low = x < 2

    rows_in(0, 0, 0, 31)
    for dst, to in ((1, back), (3, flip_y), (4, flip_z)):
        part_copy(0, 0, dst, to).start()
    rows_in(1, 0, 1, 32)
    for dst, to in ((1, back), (3, flip_y), (4, flip_z)):
        part_copy(0, 1, dst, to).start()

    def to_square(r):
        arrived(0, r)
        part_copy(0, r, 3, flip_y).start()
        part_copy(0, r, 4, flip_z).start()

    def to_back(r):
        arrived(1, r)

        @pl.when((x + 4 - step) % 4 < 2)
        def _():
            part_copy(1, r, 2, back).start()

    def to_corner(slot, r):
        arrived(slot, r)
        part_copy(slot, r, 5, flip_z if slot == 3 else flip_y).start()

    ahead_hi = (x + step) % 4 > x
    ahead_lo = jnp.logical_not(ahead_hi)
    high = jnp.logical_not(low)
    half = ROWS // 2

    def halves(a, ha, b, hb, a_hi):
        lo, hi = jnp.where(a_hi, b, a), jnp.where(a_hi, a, b)
        at_lo, at_hi = jnp.where(a_hi, hb, ha), jnp.where(a_hi, ha, hb)
        block_pair(lo, at_lo * half, half, hi, at_hi * half, half)

    def half_and_all(a, ha, b, a_hi):
        @pl.when(a_hi)
        def _():
            block_pair(b, 0, ROWS, a, ha * half, half)

        @pl.when(jnp.logical_not(a_hi))
        def _():
            block_pair(a, ha * half, half, b, 0, ROWS)

    def with_own(slot, mine_lo):
        lo = jnp.where(mine_lo, 0, slot)
        hi = jnp.where(mine_lo, slot, 0)
        block_pair(lo, jnp.where(mine_lo, 0, half), half, hi, 0, ROWS)

    def send_maxima(dst):
        to = (None, ahead, back2, flip_y, flip_z, flip_yz)[dst]
        pltpu.make_async_remote_copy(
            acc.at[dst],
            acc_got.at[dst - 1],
            acc_send.at[dst],
            acc_recv.at[dst],
            device_id=place(to),
            device_id_type=MESH,
        ).start()

    arrived(1, 2)
    part_copy(1, 2, 0, ahead).start()
    to_square(3)
    for slot in range(1, SLOTS):
        pltpu.make_async_copy(clr.at[slot], clr.at[slot], cl_recv.at[slot]).wait()
        clc[slot] = column(clr[slot, 0:1])
    to_corner(3, 0)
    to_corner(4, 1)
    to_square(2)

    @pl.loop(0, 2)
    def _(i):
        block_pair(0, 0, ROWS, 0, i * 512, 512, diag=True)

    half_and_all(1, 1, 0, ahead_hi)
    to_back(0)
    arrived(3, 1)
    arrived(4, 0)
    halves(1, 1, 3, 0, ahead_hi)
    halves(1, 1, 4, 0, ahead_hi)
    to_back(1)
    to_corner(3, 3)
    arrived(2, 3)
    for face in (0, 3, 4):
        halves(2, 1, face, 0, low)
    half_and_all(1, 0, 0, ahead_hi)
    halves(1, 0, 3, 0, ahead_hi)
    halves(1, 0, 4, 0, ahead_hi)
    to_corner(4, 2)
    arrived(3, 2)
    arrived(4, 3)
    half_and_all(3, 1, 1, ahead_lo)
    half_and_all(4, 1, 1, ahead_lo)
    with_own(3, flip_y > me)
    with_own(4, flip_z > me)

    @pl.when(high)
    def _():
        for face in (0, 3, 4):
            block_pair(2, half, half, face, half, half)

    arrived(5, 0)
    arrived(5, 1)
    half_and_all(5, 0, 1, ahead_lo)
    halves(2, 1, 5, 0, low)

    @pl.when(low)
    def _():
        arrived(2, 0)
        arrived(2, 1)
        for face in (0, 3, 4, 5):
            block_pair(face, 0, half, 2, 0, half)

    send_maxima(2)
    send_maxima(3)
    send_maxima(4)
    arrived(5, 3)
    arrived(5, 2)
    half_and_all(5, 1, 1, ahead_lo)
    with_own(5, flip_yz > me)

    @pl.when(high)
    def _():
        block_pair(2, half, half, 5, half, half)

    send_maxima(1)
    send_maxima(5)

    best = acc[0]
    for m in range(1, SLOTS):
        pltpu.make_async_copy(acc_got.at[m - 1], acc_got.at[m - 1], acc_recv.at[m]).wait()
        best = jnp.maximum(best, acc_got[m - 1])
    best = jnp.max(best, axis=0, keepdims=True)

    each = column(best).reshape(DEVS, PAIR, 128)
    each = jnp.where(iota((DEVS, PAIR, 128), 1) == iota((DEVS, PAIR, 128), 2), each, 0.0)
    ret_send[...] = jnp.sum(each, axis=1, keepdims=True)
    dev = owner * 16 + tile
    most = pl.ds(0, DEVS - 1)
    stay = pltpu.make_async_copy(ret_send.at[owner * 4 + z], ret_got.at[dev], ret_local)
    stay.start()
    for k in range(1, DEVS):
        j = k * 37 % DEVS
        o, zz = (owner + j // 4 % 8) % 8, (z + j % 4) % 4
        t = zz * 4 + (x + j // 32 * step) % 4
        pltpu.make_async_remote_copy(
            ret_send.at[j // 32 * 32 + o * 4 + zz],
            ret_got.at[dev],
            ret_sems.at[0],
            ret_sems.at[1],
            device_id=(o, t),
            device_id_type=MESH,
        ).start()
    stay.wait()
    pltpu.make_async_copy(ret_send.at[most], ret_got.at[most], ret_sems.at[1]).wait()
    got = ret_got[...].reshape(DEVS, 128)
    one = got.astype(BF16)
    rest = got - one.astype(F32)
    two = rest.astype(BF16)
    three = (rest - two.astype(F32)).astype(BF16)
    turn = turn_ref[...]
    rows = jnp.dot(one, turn, preferred_element_type=F32)
    rows = rows + jnp.dot(two, turn, preferred_element_type=F32)
    rows = rows + jnp.dot(three, turn, preferred_element_type=F32)
    out_ref[...] = jnp.sum(rows * mine_ref[...], axis=0, keepdims=True)

    left = pl.ds(0, DEVS - 3)
    pltpu.make_async_copy(send.at[left], send.at[left], send_sem).wait()
    meta_left()
    pltpu.make_async_copy(ret_send.at[most], ret_got.at[most], ret_sems.at[0]).wait()
    for c in range(CHUNKS):
        rows = pl.ds(c * CHUNK, CHUNK)
        for dst in range(SLOTS):
            if (dst, c) in ((0, 0), (0, 1), (1, 3), (2, 2)):
                continue
            sent = pltpu.make_async_copy(parts.at[0, rows], parts.at[dst, rows], copy_send.at[dst, c])
            if (dst, c) in ((2, 0), (2, 1)):
                pl.when((x + 4 - step) % 4 < 2)(sent.wait)
            else:
                sent.wait()
    for dst in range(1, SLOTS):
        pltpu.make_async_copy(clr.at[0], clr.at[dst], cl_send.at[dst]).wait()
        pltpu.make_async_copy(acc.at[dst], acc_got.at[dst - 1], acc_send.at[dst]).wait()


def per_device(embeddings, sorted_pos, block_cluster, tile_list):
    del tile_list
    vmem = pl.BlockSpec(memory_space=pltpu.VMEM)
    out = pl.pallas_call(
        kernel,
        out_shape=jax.ShapeDtypeStruct((1, ROWS), F32),
        in_specs=[pl.BlockSpec(memory_space=pl.ANY), vmem, pl.BlockSpec(memory_space=pltpu.SMEM)],
        out_specs=vmem,
        scratch_shapes=[
            pltpu.VMEM((ROWS, D), BF16),
            pltpu.VMEM((ROWS, D), BF16),
            pltpu.VMEM((ROWS, 128), F32),
            pltpu.VMEM((DEVS, PAIR, D), BF16),
            pltpu.VMEM((4, DEVS // 4, PAIR, D), BF16),
            pltpu.VMEM((SLOTS, ROWS, D), BF16),
            pltpu.VMEM((8, 128), F32),
            pltpu.VMEM((8, 128), F32),
            pltpu.VMEM((8, ROWS), F32),
            pltpu.VMEM((SLOTS, 8, ROWS), F32),
            pltpu.VMEM((SLOTS, ROWS, 128), F32),
            pltpu.VMEM((SLOTS, 8, ROWS), F32),
            pltpu.VMEM((SLOTS - 1, 8, ROWS), F32),
            pltpu.VMEM((8, 16, 1, 128), F32),
            pltpu.VMEM((8, 16, 1, 128), F32),
            pltpu.VMEM((16, 8, 1, 128), F32),
            pltpu.VMEM((DEVS, 1, 128), F32),
            pltpu.VMEM((DEVS, 1, 128), F32),
            pltpu.VMEM((1, ROWS), jnp.int32),
            pltpu.VMEM((128, ROWS), BF16),
            pltpu.VMEM((DEVS, ROWS), F32),
            pltpu.SemaphoreType.DMA,
            pltpu.SemaphoreType.DMA((4,)),
            pltpu.SemaphoreType.DMA((2,)),
            pltpu.SemaphoreType.DMA((SLOTS, CHUNKS)),
            pltpu.SemaphoreType.DMA((SLOTS, CHUNKS)),
            pltpu.SemaphoreType.DMA((SLOTS,)),
            pltpu.SemaphoreType.DMA((SLOTS,)),
            pltpu.SemaphoreType.DMA((SLOTS,)),
            pltpu.SemaphoreType.DMA((SLOTS,)),
            pltpu.SemaphoreType.DMA((2,)),
            pltpu.SemaphoreType.DMA((4,)),
            pltpu.SemaphoreType.DMA((4,)),
            pltpu.SemaphoreType.DMA,
            pltpu.SemaphoreType.DMA((2,)),
        ],
        compiler_params=pltpu.CompilerParams(
            collective_id=0, has_side_effects=True, vmem_limit_bytes=56 * 1024 * 1024
        ),
    )(embeddings, sorted_pos.reshape(1, ROWS), block_cluster)
    return out.reshape(ROWS)


def solution(mesh):
    placed = (
        P(("owner", "tile"), None),
        P(("owner", "tile")),
        P(("owner", "tile")),
        P("owner", "tile", None, None),
    )
    return jax.shard_map(
        per_device, mesh=mesh, in_specs=placed, out_specs=P(("owner", "tile")), check_vma=False
    )
```

```python
import jax
import jax.numpy as jnp
from jax import lax
from jax.experimental import pallas as pl
from jax.experimental.pallas import tpu as pltpu
from jax.sharding import PartitionSpec as P

D = 1024
BLK = 128
ROWS = 1024
DEVS = 128
PAIR = ROWS // DEVS
CHUNK = 256
CHUNKS = ROWS // CHUNK
SLOTS = 6
F32 = jnp.float32
BF16 = jnp.bfloat16
MESH = pl.DeviceIdType.MESH
NT = (((1,), (1,)), ((), ()))


def distance(j):
    return 2 * min(j // 32, 4 - j // 32) + min(j // 4 % 8, 8 - j // 4 % 8) + 2 * min(j % 4, 4 - j % 4)


FAR_FIRST = sorted(range(1, DEVS), key=lambda j: (-distance(j), j * 37 % DEVS))


def place(part):
    core = part // 64
    y = (2 * ((part // 32) % 2) + (part // 2) % 2 + core) % 4
    z = (2 * ((part // 16) % 2) + part % 2 + core) % 4
    x = (part // 4) % 4
    return y * 2 + core, z * 4 + x


def part_of(owner, tile):
    core = owner % 2
    y = (owner // 2 + 4 - core) % 4
    z = (tile // 4 + 4 - core) % 4
    x = tile % 4
    return core * 64 + (y // 2) * 32 + (z // 2) * 16 + x * 4 + (y % 2) * 2 + z % 2


def iota(shape, dim):
    return lax.broadcasted_iota(jnp.int32, shape, dim)


def rows_then_columns(sent, mid, got, owner, tile, sems, local):
    def first():
        stay = pltpu.make_async_copy(sent.at[owner], mid.at[owner], local.at[0])
        stay.start()
        for k in range(1, 8):
            to = (owner + k) % 8
            pltpu.make_async_remote_copy(
                sent.at[to],
                mid.at[owner],
                sems.at[0],
                sems.at[1],
                device_id=(to, tile),
                device_id_type=MESH,
            ).start()

    def second():
        seven = pl.ds(0, 7)
        pltpu.make_async_copy(sent.at[owner], mid.at[owner], local.at[0]).wait()
        pltpu.make_async_copy(sent.at[seven], mid.at[seven], sems.at[1]).wait()
        stay = pltpu.make_async_copy(mid.at[:, tile], got.at[tile], local.at[1])
        stay.start()
        for k in range(1, 16):
            to = (tile + k) % 16
            pltpu.make_async_remote_copy(
                mid.at[:, to],
                got.at[tile],
                sems.at[2],
                sems.at[3],
                device_id=(owner, to),
                device_id_type=MESH,
            ).start()

    def arrive():
        fifteen = pl.ds(0, 15)
        pltpu.make_async_copy(got.at[tile], got.at[tile], local.at[1]).wait()
        pltpu.make_async_copy(got.at[fifteen], got.at[fifteen], sems.at[3]).wait()

    def left():
        seven, fifteen = pl.ds(0, 7), pl.ds(0, 15)
        pltpu.make_async_copy(sent.at[seven], mid.at[seven], sems.at[0]).wait()
        pltpu.make_async_copy(got.at[fifteen], got.at[fifteen], sems.at[2]).wait()

    return first, second, arrive, left


def column(row):
    return jnp.broadcast_to(row, (128, row.shape[1])).T


def kernel(
    x_hbm,
    pos_ref,
    bc_ref,
    out_ref,
    x_ref,
    unit,
    posc,
    send,
    recv,
    parts,
    bc_here,
    bc_got,
    pos_row,
    clr,
    clc,
    acc,
    acc_got,
    meta_send,
    meta_mid,
    meta_got,
    ret_send,
    ret_got,
    rank_ref,
    turn_ref,
    mine_ref,
    send_sem,
    rows_sem,
    bc_sem,
    copy_send,
    copy_recv,
    cl_send,
    cl_recv,
    acc_send,
    acc_recv,
    ret_sems,
    meta_sems,
    keep_sem,
    ret_local,
    meta_local,
):
    owner, tile = lax.axis_index("owner"), lax.axis_index("tile")
    me = part_of(owner, tile)
    core = owner % 2
    y, z, x = owner // 2, tile // 4, tile % 4
    q = me % 4
    base = me - me % 16
    barrier = pltpu.get_barrier_semaphore()
    x_in = pltpu.make_async_copy(x_hbm, x_ref, ret_local)
    x_in.start()

    for k in range(1, DEVS):
        to = ((owner + k // 16) % 8, (tile + k % 16) % 16)
        pl.semaphore_signal(barrier, inc=1, device_id=to, device_id_type=MESH)

    pos = pos_ref[...]
    posf = pos.astype(F32)
    posc[...] = column(posf)
    ranks = []
    for t in range(ROWS // 128):
        here = posf[:, t * 128 : (t + 1) * 128]
        less = jnp.where(posc[...] < here, 1.0, 0.0)
        ranks.append(jnp.sum(less, axis=0, keepdims=True).astype(jnp.int32))
    within = jnp.concatenate(ranks, axis=1) & (PAIR - 1)
    to_o, to_t = place(pos >> 10)
    rank_ref[...] = (to_o * 16 + to_t) * PAIR + within

    x_in.wait()

    @pl.loop(0, ROWS // 128)
    def _(c):
        rows = pl.ds(pl.multiple_of(c * 128, 128), 128)
        v = x_ref[rows, :].astype(F32)
        s = lax.rsqrt(jnp.sum(v * v, axis=1, keepdims=True) + 1e-06)
        unit[rows, :] = (v * s).astype(BF16)

    @pl.loop(0, CHUNKS)
    def _(c):
        pick = jnp.where(rank_ref[...] == iota((CHUNK, ROWS), 0) + c * CHUNK, 1.0, 0.0).astype(BF16)
        got = jnp.dot(pick, unit[...], preferred_element_type=F32)
        blocks = CHUNK // PAIR
        send[pl.ds(c * blocks, blocks)] = got.reshape(blocks, PAIR, D).astype(BF16)

    inside = pos & (ROWS - 1)
    here = iota((DEVS, ROWS), 0) == to_o * 16 + to_t
    high = jnp.where(here, (inside >> 5).astype(F32), 0.0).astype(BF16)
    below = jnp.where(here, (inside & 31).astype(F32), 0.0).astype(BF16)
    lane = iota((128, ROWS), 0)
    turn = jnp.where(lane == within, 1.0, 0.0).astype(BF16)
    turn2 = jnp.where(lane == within + PAIR, 1.0, 0.0).astype(BF16)
    meta = lax.dot_general(high, turn, NT, preferred_element_type=F32)
    meta = meta + lax.dot_general(below, turn2, NT, preferred_element_type=F32)
    meta_send[...] = meta.reshape(8, 16, 1, 128)
    turn_ref[...] = turn
    mine_ref[...] = jnp.where(here, 1.0, 0.0)

    for b in range(ROWS // BLK):
        bc_here[b : b + 1, :] = jnp.full((1, 128), bc_ref[b], jnp.int32).astype(F32)

    pl.semaphore_wait(barrier, DEVS - 1)

    listed = owner * 16 + tile

    @pl.when(listed != me)
    def _():
        pltpu.make_async_remote_copy(
            bc_here, bc_got, bc_sem.at[0], bc_sem.at[1], device_id=place(listed), device_id_type=MESH
        ).start()

    @pl.when(listed == me)
    def _():
        pltpu.make_async_copy(bc_here, bc_got, bc_sem.at[1]).start()

    step = jnp.where(core == 0, 1, 3)

    def send_rows(r, block, first):
        @pl.loop(first, 32)
        def _(k):
            j = k * 13 % 32
            o, zz = (owner + j // 4) % 8, (z + j) % 4
            column_of = (x + r * (4 - (1 + 2 * (o % 2)))) % 4
            to_x = column_of if r == 1 else x
            pltpu.make_async_remote_copy(
                send.at[o * 16 + zz * 4 + column_of],
                recv.at[block, owner * 4 + z],
                send_sem,
                rows_sem.at[block],
                device_id=(o, zz * 4 + to_x),
                device_id_type=MESH,
            ).start()

    def keep_rows(r, block):
        column_of = (x + r * (4 - step)) % 4
        return pltpu.make_async_copy(
            send.at[owner * 16 + z * 4 + column_of], recv.at[block, owner * 4 + z], keep_sem.at[block]
        )

    meta_first, meta_second, meta_arrive, meta_left = rows_then_columns(
        meta_send, meta_mid, meta_got, owner, tile, meta_sems, meta_local
    )
    meta_first()
    keep_rows(2, 3).start()
    keep_rows(3, 2).start()
    keep_rows(0, 0).start()
    send_rows(2, 3, 1)
    meta_second()
    send_rows(3, 2, 1)
    send_rows(0, 0, 1)
    send_rows(1, 1, 0)

    back = base + ((x + 4 - step) % 4) * 4 + q
    back2 = base + ((x + 2) % 4) * 4 + q
    ahead = base + ((x + step) % 4) * 4 + q
    flip_y = me - q + (q + 2) % 4
    flip_z = me - q + (q // 2) * 2 + (q + 1) % 2
    flip_yz = me - q + 3 - q

    meta_arrive()
    pltpu.make_async_copy(bc_here, bc_got, bc_sem.at[1]).wait()

    @pl.when(listed != me)
    def _():
        pltpu.make_async_copy(bc_here, bc_got, bc_sem.at[0]).wait()

    got = meta_got[...].reshape(DEVS, 128).astype(BF16)
    lane, at = iota((128, ROWS), 0), iota((128, ROWS), 1)
    turn = jnp.where(lane == (at & 7), 32.0, jnp.where(lane == (at & 7) + PAIR, 1.0, 0.0)).astype(BF16)
    at_row = jnp.dot(got, turn, preferred_element_type=F32)
    source = iota((DEVS, ROWS), 1) >> 3
    source_x = (x + (source >> 5) * step) & 3
    source = ((source & 3) * 4 + source_x) * 8 + ((source >> 2) & 7)
    at_row = jnp.where(source == iota((DEVS, ROWS), 0), at_row, 0.0)
    own_pos = jnp.sum(at_row, axis=0, keepdims=True)
    pos_row[...] = jnp.broadcast_to(own_pos, (8, ROWS))
    block = own_pos.astype(jnp.int32) >> 7
    own_cl = jnp.zeros((1, ROWS), F32)
    for b in range(ROWS // BLK):
        own_cl = own_cl + jnp.where(block == b, bc_got[b : b + 1, 0:1], 0.0)
    clr[0] = jnp.broadcast_to(own_cl, (8, ROWS))
    for dst, to in ((1, back), (2, back2), (3, flip_y), (4, flip_z), (5, flip_yz)):
        pltpu.make_async_remote_copy(
            clr.at[0], clr.at[dst], cl_send.at[dst], cl_recv.at[dst], device_id=place(to), device_id_type=MESH
        ).start()
    clc[0] = column(own_cl)
    posc[...] = column(own_pos)
    for m in range(SLOTS):
        acc[m] = jnp.full((8, ROWS), -1.0, F32)

    def part_copy(src, c, dst, to):
        rows = pl.ds(c * CHUNK, CHUNK)
        return pltpu.make_async_remote_copy(
            parts.at[src, rows],
            parts.at[dst, rows],
            copy_send.at[dst, c],
            copy_recv.at[dst, c],
            device_id=place(to),
            device_id_type=MESH,
        )

    def arrived(slot, c):
        rows = pl.ds(c * CHUNK, CHUNK)
        pltpu.make_async_copy(parts.at[slot, rows], parts.at[slot, rows], copy_recv.at[slot, c]).wait()

    def rows_in(block, slot, r, remote):
        most = pl.ds(0, remote)
        pltpu.make_async_copy(recv.at[block, most], recv.at[block, most], rows_sem.at[block]).wait()
        if remote < 32:
            keep_rows(r, block).wait()
        rows = pl.ds(r * CHUNK, CHUNK)
        parts[slot, rows, :] = recv[block].astype(F32).reshape(CHUNK, D).astype(BF16)

    rows_in(3, 2, 2, 31)
    part_copy(2, 2, 1, ahead).start()
    rows_in(2, 1, 3, 31)
    part_copy(1, 3, 0, ahead).start()
    part_copy(1, 3, 2, back).start()

    def fold(s, mask, hi, cols):
        kept = jnp.where(mask, s, -1.0)
        top = jnp.max(kept.reshape(kept.shape[0] // 8, 8, kept.shape[1]), axis=0)
        acc[hi, :, cols] = jnp.maximum(acc[hi, :, cols], top)

    def block_pair(lo, row, m, hi, col, n, diag=False):
        rows = pl.ds(pl.multiple_of(row, m), m)
        cols = pl.ds(pl.multiple_of(col, n), n)
        s = lax.dot_general(parts[lo, rows, :], parts[hi, cols, :], NT, preferred_element_type=F32)
        for k in range(n // 128):
            at = pl.ds(pl.multiple_of(col + k * 128, 128), 128)
            mask = clc[lo, rows, :] == clr[hi, 0:1, at]
            if diag:
                mask = mask & (posc[rows, :] < pos_row[0:1, at])
            fold(s[:, k * 128 : (k + 1) * 128], mask, hi, at)

    low = x < 2

    rows_in(0, 0, 0, 31)
    for dst, to in ((1, back), (3, flip_y), (4, flip_z)):
        part_copy(0, 0, dst, to).start()
    rows_in(1, 0, 1, 32)
    for dst, to in ((1, back), (3, flip_y), (4, flip_z)):
        part_copy(0, 1, dst, to).start()

    def to_square(r):
        arrived(0, r)
        part_copy(0, r, 3, flip_y).start()
        part_copy(0, r, 4, flip_z).start()

    def to_back(r):
        arrived(1, r)

        @pl.when((x + 4 - step) % 4 < 2)
        def _():
            part_copy(1, r, 2, back).start()

    def to_corner(slot, r):
        arrived(slot, r)
        part_copy(slot, r, 5, flip_z if slot == 3 else flip_y).start()

    ahead_hi = (x + step) % 4 > x
    ahead_lo = jnp.logical_not(ahead_hi)
    high = jnp.logical_not(low)
    half = ROWS // 2

    def halves(a, ha, b, hb, a_hi):
        lo, hi = jnp.where(a_hi, b, a), jnp.where(a_hi, a, b)
        at_lo, at_hi = jnp.where(a_hi, hb, ha), jnp.where(a_hi, ha, hb)
        block_pair(lo, at_lo * half, half, hi, at_hi * half, half)

    def half_and_all(a, ha, b, a_hi):
        @pl.when(a_hi)
        def _():
            block_pair(b, 0, ROWS, a, ha * half, half)

        @pl.when(jnp.logical_not(a_hi))
        def _():
            block_pair(a, ha * half, half, b, 0, ROWS)

    def with_own(slot, mine_lo):
        lo = jnp.where(mine_lo, 0, slot)
        hi = jnp.where(mine_lo, slot, 0)
        block_pair(lo, jnp.where(mine_lo, 0, half), half, hi, 0, ROWS)

    def send_maxima(dst):
        to = (None, ahead, back2, flip_y, flip_z, flip_yz)[dst]
        pltpu.make_async_remote_copy(
            acc.at[dst],
            acc_got.at[dst - 1],
            acc_send.at[dst],
            acc_recv.at[dst],
            device_id=place(to),
            device_id_type=MESH,
        ).start()

    arrived(1, 2)
    part_copy(1, 2, 0, ahead).start()
    to_square(3)
    for slot in range(1, SLOTS):
        pltpu.make_async_copy(clr.at[slot], clr.at[slot], cl_recv.at[slot]).wait()
        clc[slot] = column(clr[slot, 0:1])
    to_corner(3, 0)
    halves(1, 1, 0, 0, ahead_hi)
    to_corner(4, 1)
    arrived(2, 3)
    halves(2, 1, 0, 0, low)
    to_square(2)

    @pl.loop(0, 2)
    def _(i):
        block_pair(0, 0, ROWS, 0, i * 512, 512, diag=True)

    halves(1, 1, 0, 1, ahead_hi)
    to_back(0)
    arrived(3, 1)
    arrived(4, 0)
    halves(1, 1, 3, 0, ahead_hi)
    halves(1, 1, 4, 0, ahead_hi)
    to_back(1)
    to_corner(3, 3)
    for face in (3, 4):
        halves(2, 1, face, 0, low)
    half_and_all(1, 0, 0, ahead_hi)
    halves(1, 0, 3, 0, ahead_hi)
    halves(1, 0, 4, 0, ahead_hi)
    to_corner(4, 2)
    arrived(3, 2)
    arrived(4, 3)
    half_and_all(3, 1, 1, ahead_lo)
    half_and_all(4, 1, 1, ahead_lo)
    with_own(3, flip_y > me)
    with_own(4, flip_z > me)

    @pl.when(high)
    def _():
        for face in (0, 3, 4):
            block_pair(2, half, half, face, half, half)

    arrived(5, 0)
    arrived(5, 1)
    half_and_all(5, 0, 1, ahead_lo)
    halves(2, 1, 5, 0, low)

    @pl.when(low)
    def _():
        arrived(2, 0)
        arrived(2, 1)
        for face in (0, 3, 4, 5):
            block_pair(face, 0, half, 2, 0, half)

    send_maxima(2)
    send_maxima(3)
    send_maxima(4)
    arrived(5, 3)
    arrived(5, 2)
    half_and_all(5, 1, 1, ahead_lo)
    send_maxima(1)
    with_own(5, flip_yz > me)

    @pl.when(high)
    def _():
        block_pair(2, half, half, 5, half, half)

    send_maxima(5)

    best = acc[0]
    for m in range(1, SLOTS):
        pltpu.make_async_copy(acc_got.at[m - 1], acc_got.at[m - 1], acc_recv.at[m]).wait()
        best = jnp.maximum(best, acc_got[m - 1])
    best = jnp.max(best, axis=0, keepdims=True)

    each = column(best).reshape(DEVS, PAIR, 128)
    each = jnp.where(iota((DEVS, PAIR, 128), 1) == iota((DEVS, PAIR, 128), 2), each, 0.0)
    ret_send[...] = jnp.sum(each, axis=1, keepdims=True)
    dev = owner * 16 + tile
    most = pl.ds(0, DEVS - 1)
    stay = pltpu.make_async_copy(ret_send.at[owner * 4 + z], ret_got.at[dev], ret_local)
    stay.start()
    for j in FAR_FIRST:
        o, zz = (owner + j // 4 % 8) % 8, (z + j % 4) % 4
        t = zz * 4 + (x + j // 32 * step) % 4
        pltpu.make_async_remote_copy(
            ret_send.at[j // 32 * 32 + o * 4 + zz],
            ret_got.at[dev],
            ret_sems.at[0],
            ret_sems.at[1],
            device_id=(o, t),
            device_id_type=MESH,
        ).start()
    stay.wait()
    pltpu.make_async_copy(ret_send.at[most], ret_got.at[most], ret_sems.at[1]).wait()
    got = ret_got[...].reshape(DEVS, 128)
    one = got.astype(BF16)
    rest = got - one.astype(F32)
    two = rest.astype(BF16)
    three = (rest - two.astype(F32)).astype(BF16)
    turn = turn_ref[...]
    rows = jnp.dot(one, turn, preferred_element_type=F32)
    rows = rows + jnp.dot(two, turn, preferred_element_type=F32)
    rows = rows + jnp.dot(three, turn, preferred_element_type=F32)
    out_ref[...] = jnp.sum(rows * mine_ref[...], axis=0, keepdims=True)

    left = pl.ds(0, DEVS - 3)
    pltpu.make_async_copy(send.at[left], send.at[left], send_sem).wait()
    meta_left()
    pltpu.make_async_copy(ret_send.at[most], ret_got.at[most], ret_sems.at[0]).wait()
    for c in range(CHUNKS):
        rows = pl.ds(c * CHUNK, CHUNK)
        for dst in range(SLOTS):
            if (dst, c) in ((0, 0), (0, 1), (1, 3), (2, 2)):
                continue
            sent = pltpu.make_async_copy(parts.at[0, rows], parts.at[dst, rows], copy_send.at[dst, c])
            if (dst, c) in ((2, 0), (2, 1)):
                pl.when((x + 4 - step) % 4 < 2)(sent.wait)
            else:
                sent.wait()
    for dst in range(1, SLOTS):
        pltpu.make_async_copy(clr.at[0], clr.at[dst], cl_send.at[dst]).wait()
        pltpu.make_async_copy(acc.at[dst], acc_got.at[dst - 1], acc_send.at[dst]).wait()


def per_device(embeddings, sorted_pos, block_cluster, tile_list):
    del tile_list
    vmem = pl.BlockSpec(memory_space=pltpu.VMEM)
    out = pl.pallas_call(
        kernel,
        out_shape=jax.ShapeDtypeStruct((1, ROWS), F32),
        in_specs=[pl.BlockSpec(memory_space=pl.ANY), vmem, pl.BlockSpec(memory_space=pltpu.SMEM)],
        out_specs=vmem,
        scratch_shapes=[
            pltpu.VMEM((ROWS, D), BF16),
            pltpu.VMEM((ROWS, D), BF16),
            pltpu.VMEM((ROWS, 128), F32),
            pltpu.VMEM((DEVS, PAIR, D), BF16),
            pltpu.VMEM((4, DEVS // 4, PAIR, D), BF16),
            pltpu.VMEM((SLOTS, ROWS, D), BF16),
            pltpu.VMEM((8, 128), F32),
            pltpu.VMEM((8, 128), F32),
            pltpu.VMEM((8, ROWS), F32),
            pltpu.VMEM((SLOTS, 8, ROWS), F32),
            pltpu.VMEM((SLOTS, ROWS, 128), F32),
            pltpu.VMEM((SLOTS, 8, ROWS), F32),
            pltpu.VMEM((SLOTS - 1, 8, ROWS), F32),
            pltpu.VMEM((8, 16, 1, 128), F32),
            pltpu.VMEM((8, 16, 1, 128), F32),
            pltpu.VMEM((16, 8, 1, 128), F32),
            pltpu.VMEM((DEVS, 1, 128), F32),
            pltpu.VMEM((DEVS, 1, 128), F32),
            pltpu.VMEM((1, ROWS), jnp.int32),
            pltpu.VMEM((128, ROWS), BF16),
            pltpu.VMEM((DEVS, ROWS), F32),
            pltpu.SemaphoreType.DMA,
            pltpu.SemaphoreType.DMA((4,)),
            pltpu.SemaphoreType.DMA((2,)),
            pltpu.SemaphoreType.DMA((SLOTS, CHUNKS)),
            pltpu.SemaphoreType.DMA((SLOTS, CHUNKS)),
            pltpu.SemaphoreType.DMA((SLOTS,)),
            pltpu.SemaphoreType.DMA((SLOTS,)),
            pltpu.SemaphoreType.DMA((SLOTS,)),
            pltpu.SemaphoreType.DMA((SLOTS,)),
            pltpu.SemaphoreType.DMA((2,)),
            pltpu.SemaphoreType.DMA((4,)),
            pltpu.SemaphoreType.DMA((4,)),
            pltpu.SemaphoreType.DMA,
            pltpu.SemaphoreType.DMA((2,)),
        ],
        compiler_params=pltpu.CompilerParams(
            collective_id=0, has_side_effects=True, vmem_limit_bytes=56 * 1024 * 1024
        ),
    )(embeddings, sorted_pos.reshape(1, ROWS), block_cluster)
    return out.reshape(ROWS)


def solution(mesh):
    placed = (
        P(("owner", "tile"), None),
        P(("owner", "tile")),
        P(("owner", "tile")),
        P("owner", "tile", None, None),
    )
    return jax.shard_map(
        per_device, mesh=mesh, in_specs=placed, out_specs=P(("owner", "tile")), check_vma=False
    )
```

```python
import jax
import jax.numpy as jnp
from jax import lax
from jax.experimental import pallas as pl
from jax.experimental.pallas import tpu as pltpu
from jax.sharding import PartitionSpec as P

D = 1024
BLK = 128
ROWS = 1024
DEVS = 128
PAIR = ROWS // DEVS
CHUNK = 256
CHUNKS = ROWS // CHUNK
SLOTS = 6
F32 = jnp.float32
BF16 = jnp.bfloat16
MESH = pl.DeviceIdType.MESH
NT = (((1,), (1,)), ((), ()))


def distance(j):
    return 2 * min(j // 32, 4 - j // 32) + min(j // 4 % 8, 8 - j // 4 % 8) + 2 * min(j % 4, 4 - j % 4)


FAR_FIRST = sorted(range(1, DEVS), key=lambda j: (-distance(j), j * 37 % DEVS))


def place(part):
    core = part // 64
    y = (2 * ((part // 32) % 2) + (part // 2) % 2 + core) % 4
    z = (2 * ((part // 16) % 2) + part % 2 + core) % 4
    x = (part // 4) % 4
    return y * 2 + core, z * 4 + x


def part_of(owner, tile):
    core = owner % 2
    y = (owner // 2 + 4 - core) % 4
    z = (tile // 4 + 4 - core) % 4
    x = tile % 4
    return core * 64 + (y // 2) * 32 + (z // 2) * 16 + x * 4 + (y % 2) * 2 + z % 2


def iota(shape, dim):
    return lax.broadcasted_iota(jnp.int32, shape, dim)


def rows_then_columns(sent, mid, got, owner, tile, sems, local):
    def first():
        stay = pltpu.make_async_copy(sent.at[owner], mid.at[owner], local.at[0])
        stay.start()
        for k in range(1, 8):
            to = (owner + k) % 8
            pltpu.make_async_remote_copy(
                sent.at[to],
                mid.at[owner],
                sems.at[0],
                sems.at[1],
                device_id=(to, tile),
                device_id_type=MESH,
            ).start()

    def second():
        seven = pl.ds(0, 7)
        pltpu.make_async_copy(sent.at[owner], mid.at[owner], local.at[0]).wait()
        pltpu.make_async_copy(sent.at[seven], mid.at[seven], sems.at[1]).wait()
        stay = pltpu.make_async_copy(mid.at[:, tile], got.at[tile], local.at[1])
        stay.start()
        for k in range(1, 16):
            to = (tile + k) % 16
            pltpu.make_async_remote_copy(
                mid.at[:, to],
                got.at[tile],
                sems.at[2],
                sems.at[3],
                device_id=(owner, to),
                device_id_type=MESH,
            ).start()

    def arrive():
        fifteen = pl.ds(0, 15)
        pltpu.make_async_copy(got.at[tile], got.at[tile], local.at[1]).wait()
        pltpu.make_async_copy(got.at[fifteen], got.at[fifteen], sems.at[3]).wait()

    def left():
        seven, fifteen = pl.ds(0, 7), pl.ds(0, 15)
        pltpu.make_async_copy(sent.at[seven], mid.at[seven], sems.at[0]).wait()
        pltpu.make_async_copy(got.at[fifteen], got.at[fifteen], sems.at[2]).wait()

    return first, second, arrive, left


def column(row):
    return jnp.broadcast_to(row, (128, row.shape[1])).T


def kernel(
    x_hbm,
    pos_ref,
    bc_ref,
    out_ref,
    x_ref,
    unit,
    posc,
    send,
    recv,
    parts,
    bc_here,
    bc_got,
    pos_row,
    clr,
    clc,
    acc,
    acc_got,
    meta_send,
    meta_mid,
    meta_got,
    ret_send,
    ret_got,
    rank_ref,
    turn_ref,
    mine_ref,
    send_sem,
    rows_sem,
    bc_sem,
    copy_send,
    copy_recv,
    cl_send,
    cl_recv,
    acc_send,
    acc_recv,
    ret_sems,
    meta_sems,
    keep_sem,
    ret_local,
    meta_local,
):
    owner, tile = lax.axis_index("owner"), lax.axis_index("tile")
    me = part_of(owner, tile)
    core = owner % 2
    y, z, x = owner // 2, tile // 4, tile % 4
    q = me % 4
    base = me - me % 16
    barrier = pltpu.get_barrier_semaphore()
    x_in = pltpu.make_async_copy(x_hbm, x_ref, ret_local)
    x_in.start()

    for k in range(1, DEVS):
        to = ((owner + k // 16) % 8, (tile + k % 16) % 16)
        pl.semaphore_signal(barrier, inc=1, device_id=to, device_id_type=MESH)

    pos = pos_ref[...]
    posf = pos.astype(F32)
    posc[...] = column(posf)
    ranks = []
    for t in range(ROWS // 128):
        here = posf[:, t * 128 : (t + 1) * 128]
        less = jnp.where(posc[...] < here, 1.0, 0.0)
        ranks.append(jnp.sum(less, axis=0, keepdims=True).astype(jnp.int32))
    within = jnp.concatenate(ranks, axis=1) & (PAIR - 1)
    to_o, to_t = place(pos >> 10)
    rank_ref[...] = (to_o * 16 + to_t) * PAIR + within

    x_in.wait()

    @pl.loop(0, ROWS // 128)
    def _(c):
        rows = pl.ds(pl.multiple_of(c * 128, 128), 128)
        v = x_ref[rows, :].astype(F32)
        s = lax.rsqrt(jnp.sum(v * v, axis=1, keepdims=True) + 1e-06)
        unit[rows, :] = (v * s).astype(BF16)

    @pl.loop(0, CHUNKS)
    def _(c):
        pick = jnp.where(rank_ref[...] == iota((CHUNK, ROWS), 0) + c * CHUNK, 1.0, 0.0).astype(BF16)
        got = jnp.dot(pick, unit[...], preferred_element_type=F32)
        blocks = CHUNK // PAIR
        send[pl.ds(c * blocks, blocks)] = got.reshape(blocks, PAIR, D).astype(BF16)

    inside = pos & (ROWS - 1)
    here = iota((DEVS, ROWS), 0) == to_o * 16 + to_t
    high = jnp.where(here, (inside >> 5).astype(F32), 0.0).astype(BF16)
    below = jnp.where(here, (inside & 31).astype(F32), 0.0).astype(BF16)
    lane = iota((128, ROWS), 0)
    turn = jnp.where(lane == within, 1.0, 0.0).astype(BF16)
    turn2 = jnp.where(lane == within + PAIR, 1.0, 0.0).astype(BF16)
    meta = lax.dot_general(high, turn, NT, preferred_element_type=F32)
    meta = meta + lax.dot_general(below, turn2, NT, preferred_element_type=F32)
    meta_send[...] = meta.reshape(8, 16, 1, 128)
    turn_ref[...] = turn
    mine_ref[...] = jnp.where(here, 1.0, 0.0)

    for b in range(ROWS // BLK):
        bc_here[b : b + 1, :] = jnp.full((1, 128), bc_ref[b], jnp.int32).astype(F32)

    pl.semaphore_wait(barrier, DEVS - 1)

    listed = owner * 16 + tile

    @pl.when(listed != me)
    def _():
        pltpu.make_async_remote_copy(
            bc_here, bc_got, bc_sem.at[0], bc_sem.at[1], device_id=place(listed), device_id_type=MESH
        ).start()

    @pl.when(listed == me)
    def _():
        pltpu.make_async_copy(bc_here, bc_got, bc_sem.at[1]).start()

    step = jnp.where(core == 0, 1, 3)

    def send_rows(r, block, first):
        @pl.loop(first, 32)
        def _(k):
            j = k * 11 % 32
            o, zz = (owner + j // 4) % 8, (z + j) % 4
            column_of = (x + r * (4 - (1 + 2 * (o % 2)))) % 4
            to_x = column_of if r == 1 else x
            pltpu.make_async_remote_copy(
                send.at[o * 16 + zz * 4 + column_of],
                recv.at[block, owner * 4 + z],
                send_sem,
                rows_sem.at[block],
                device_id=(o, zz * 4 + to_x),
                device_id_type=MESH,
            ).start()

    def keep_rows(r, block):
        column_of = (x + r * (4 - step)) % 4
        return pltpu.make_async_copy(
            send.at[owner * 16 + z * 4 + column_of], recv.at[block, owner * 4 + z], keep_sem.at[block]
        )

    meta_first, meta_second, meta_arrive, meta_left = rows_then_columns(
        meta_send, meta_mid, meta_got, owner, tile, meta_sems, meta_local
    )
    meta_first()
    keep_rows(2, 3).start()
    keep_rows(3, 2).start()
    keep_rows(0, 0).start()
    send_rows(2, 3, 1)
    meta_second()
    send_rows(3, 2, 1)
    send_rows(0, 0, 1)
    send_rows(1, 1, 0)

    back = base + ((x + 4 - step) % 4) * 4 + q
    back2 = base + ((x + 2) % 4) * 4 + q
    ahead = base + ((x + step) % 4) * 4 + q
    flip_y = me - q + (q + 2) % 4
    flip_z = me - q + (q // 2) * 2 + (q + 1) % 2
    flip_yz = me - q + 3 - q

    meta_arrive()
    pltpu.make_async_copy(bc_here, bc_got, bc_sem.at[1]).wait()

    @pl.when(listed != me)
    def _():
        pltpu.make_async_copy(bc_here, bc_got, bc_sem.at[0]).wait()

    got = meta_got[...].reshape(DEVS, 128).astype(BF16)
    lane, at = iota((128, ROWS), 0), iota((128, ROWS), 1)
    turn = jnp.where(lane == (at & 7), 32.0, jnp.where(lane == (at & 7) + PAIR, 1.0, 0.0)).astype(BF16)
    at_row = jnp.dot(got, turn, preferred_element_type=F32)
    source = iota((DEVS, ROWS), 1) >> 3
    source_x = (x + (source >> 5) * step) & 3
    source = ((source & 3) * 4 + source_x) * 8 + ((source >> 2) & 7)
    at_row = jnp.where(source == iota((DEVS, ROWS), 0), at_row, 0.0)
    own_pos = jnp.sum(at_row, axis=0, keepdims=True)
    pos_row[...] = jnp.broadcast_to(own_pos, (8, ROWS))
    block = own_pos.astype(jnp.int32) >> 7
    own_cl = jnp.zeros((1, ROWS), F32)
    for b in range(ROWS // BLK):
        own_cl = own_cl + jnp.where(block == b, bc_got[b : b + 1, 0:1], 0.0)
    clr[0] = jnp.broadcast_to(own_cl, (8, ROWS))
    for dst, to in ((1, back), (2, back2), (3, flip_y), (4, flip_z), (5, flip_yz)):
        pltpu.make_async_remote_copy(
            clr.at[0], clr.at[dst], cl_send.at[dst], cl_recv.at[dst], device_id=place(to), device_id_type=MESH
        ).start()
    clc[0] = column(own_cl)
    posc[...] = column(own_pos)
    for m in range(SLOTS):
        acc[m] = jnp.full((8, ROWS), -1.0, F32)

    def part_copy(src, c, dst, to):
        rows = pl.ds(c * CHUNK, CHUNK)
        return pltpu.make_async_remote_copy(
            parts.at[src, rows],
            parts.at[dst, rows],
            copy_send.at[dst, c],
            copy_recv.at[dst, c],
            device_id=place(to),
            device_id_type=MESH,
        )

    def arrived(slot, c):
        rows = pl.ds(c * CHUNK, CHUNK)
        pltpu.make_async_copy(parts.at[slot, rows], parts.at[slot, rows], copy_recv.at[slot, c]).wait()

    def rows_in(block, slot, r, remote):
        most = pl.ds(0, remote)
        pltpu.make_async_copy(recv.at[block, most], recv.at[block, most], rows_sem.at[block]).wait()
        if remote < 32:
            keep_rows(r, block).wait()
        rows = pl.ds(r * CHUNK, CHUNK)
        parts[slot, rows, :] = recv[block].astype(F32).reshape(CHUNK, D).astype(BF16)

    rows_in(3, 2, 2, 31)
    part_copy(2, 2, 1, ahead).start()
    rows_in(2, 1, 3, 31)
    part_copy(1, 3, 0, ahead).start()
    part_copy(1, 3, 2, back).start()

    def fold(s, mask, hi, cols):
        kept = jnp.where(mask, s, -1.0)
        top = jnp.max(kept.reshape(kept.shape[0] // 8, 8, kept.shape[1]), axis=0)
        acc[hi, :, cols] = jnp.maximum(acc[hi, :, cols], top)

    def block_pair(lo, row, m, hi, col, n, diag=False):
        rows = pl.ds(pl.multiple_of(row, m), m)
        cols = pl.ds(pl.multiple_of(col, n), n)
        s = lax.dot_general(parts[lo, rows, :], parts[hi, cols, :], NT, preferred_element_type=F32)
        for k in range(n // 128):
            at = pl.ds(pl.multiple_of(col + k * 128, 128), 128)
            mask = clc[lo, rows, :] == clr[hi, 0:1, at]
            if diag:
                mask = mask & (posc[rows, :] < pos_row[0:1, at])
            fold(s[:, k * 128 : (k + 1) * 128], mask, hi, at)

    low = x < 2

    rows_in(0, 0, 0, 31)
    for dst, to in ((1, back), (3, flip_y), (4, flip_z)):
        part_copy(0, 0, dst, to).start()
    rows_in(1, 0, 1, 32)
    for dst, to in ((1, back), (3, flip_y), (4, flip_z)):
        part_copy(0, 1, dst, to).start()

    def to_square(r):
        arrived(0, r)
        part_copy(0, r, 3, flip_y).start()
        part_copy(0, r, 4, flip_z).start()

    def to_back(r):
        arrived(1, r)

        @pl.when((x + 4 - step) % 4 < 2)
        def _():
            part_copy(1, r, 2, back).start()

    def to_corner(slot, r):
        arrived(slot, r)
        part_copy(slot, r, 5, flip_z if slot == 3 else flip_y).start()

    ahead_hi = (x + step) % 4 > x
    ahead_lo = jnp.logical_not(ahead_hi)
    high = jnp.logical_not(low)
    half = ROWS // 2

    def halves(a, ha, b, hb, a_hi):
        lo, hi = jnp.where(a_hi, b, a), jnp.where(a_hi, a, b)
        at_lo, at_hi = jnp.where(a_hi, hb, ha), jnp.where(a_hi, ha, hb)
        block_pair(lo, at_lo * half, half, hi, at_hi * half, half)

    def half_and_all(a, ha, b, a_hi):
        @pl.when(a_hi)
        def _():
            block_pair(b, 0, ROWS, a, ha * half, half)

        @pl.when(jnp.logical_not(a_hi))
        def _():
            block_pair(a, ha * half, half, b, 0, ROWS)

    def with_own(slot, mine_lo):
        lo = jnp.where(mine_lo, 0, slot)
        hi = jnp.where(mine_lo, slot, 0)
        block_pair(lo, jnp.where(mine_lo, 0, half), half, hi, 0, ROWS)

    def send_maxima(dst):
        to = (None, ahead, back2, flip_y, flip_z, flip_yz)[dst]
        pltpu.make_async_remote_copy(
            acc.at[dst],
            acc_got.at[dst - 1],
            acc_send.at[dst],
            acc_recv.at[dst],
            device_id=place(to),
            device_id_type=MESH,
        ).start()

    def clusters_in(*slots):
        for slot in slots:
            pltpu.make_async_copy(clr.at[slot], clr.at[slot], cl_recv.at[slot]).wait()
            clc[slot] = column(clr[slot, 0:1])

    arrived(1, 2)
    part_copy(1, 2, 0, ahead).start()
    to_square(3)
    clusters_in(1, 2)
    to_corner(3, 0)
    halves(1, 1, 0, 0, ahead_hi)
    to_corner(4, 1)
    arrived(2, 3)
    halves(2, 1, 0, 0, low)
    to_square(2)
    clusters_in(3, 4, 5)

    @pl.loop(0, 2)
    def _(i):
        block_pair(0, 0, ROWS, 0, i * 512, 512, diag=True)

    halves(1, 1, 0, 1, ahead_hi)
    to_back(0)
    arrived(3, 1)
    arrived(4, 0)
    halves(1, 1, 3, 0, ahead_hi)
    halves(1, 1, 4, 0, ahead_hi)
    to_back(1)
    to_corner(3, 3)
    for face in (3, 4):
        halves(2, 1, face, 0, low)
    half_and_all(1, 0, 0, ahead_hi)
    halves(1, 0, 3, 0, ahead_hi)
    halves(1, 0, 4, 0, ahead_hi)
    to_corner(4, 2)
    arrived(3, 2)
    arrived(4, 3)
    half_and_all(3, 1, 1, ahead_lo)
    half_and_all(4, 1, 1, ahead_lo)
    with_own(3, flip_y > me)
    with_own(4, flip_z > me)

    @pl.when(high)
    def _():
        for face in (0, 3, 4):
            block_pair(2, half, half, face, half, half)

    arrived(5, 0)
    arrived(5, 1)
    half_and_all(5, 0, 1, ahead_lo)
    halves(2, 1, 5, 0, low)

    @pl.when(low)
    def _():
        arrived(2, 0)
        arrived(2, 1)
        for face in (0, 3, 4, 5):
            block_pair(face, 0, half, 2, 0, half)

    send_maxima(2)
    send_maxima(3)
    send_maxima(4)
    arrived(5, 3)
    arrived(5, 2)
    half_and_all(5, 1, 1, ahead_lo)
    send_maxima(1)
    with_own(5, flip_yz > me)

    @pl.when(high)
    def _():
        block_pair(2, half, half, 5, half, half)

    send_maxima(5)

    best = acc[0]
    for m in range(1, SLOTS):
        pltpu.make_async_copy(acc_got.at[m - 1], acc_got.at[m - 1], acc_recv.at[m]).wait()
        best = jnp.maximum(best, acc_got[m - 1])
    best = jnp.max(best, axis=0, keepdims=True)

    each = column(best).reshape(DEVS, PAIR, 128)
    each = jnp.where(iota((DEVS, PAIR, 128), 1) == iota((DEVS, PAIR, 128), 2), each, 0.0)
    ret_send[...] = jnp.sum(each, axis=1, keepdims=True)
    dev = owner * 16 + tile
    most = pl.ds(0, DEVS - 1)
    stay = pltpu.make_async_copy(ret_send.at[owner * 4 + z], ret_got.at[dev], ret_local)
    stay.start()
    for j in FAR_FIRST:
        o, zz = (owner + j // 4 % 8) % 8, (z + j % 4) % 4
        t = zz * 4 + (x + j // 32 * step) % 4
        pltpu.make_async_remote_copy(
            ret_send.at[j // 32 * 32 + o * 4 + zz],
            ret_got.at[dev],
            ret_sems.at[0],
            ret_sems.at[1],
            device_id=(o, t),
            device_id_type=MESH,
        ).start()
    stay.wait()
    pltpu.make_async_copy(ret_send.at[most], ret_got.at[most], ret_sems.at[1]).wait()
    got = ret_got[...].reshape(DEVS, 128)
    one = got.astype(BF16)
    rest = got - one.astype(F32)
    two = rest.astype(BF16)
    three = (rest - two.astype(F32)).astype(BF16)
    turn = turn_ref[...]
    rows = jnp.dot(one, turn, preferred_element_type=F32)
    rows = rows + jnp.dot(two, turn, preferred_element_type=F32)
    rows = rows + jnp.dot(three, turn, preferred_element_type=F32)
    out_ref[...] = jnp.sum(rows * mine_ref[...], axis=0, keepdims=True)

    left = pl.ds(0, DEVS - 3)
    pltpu.make_async_copy(send.at[left], send.at[left], send_sem).wait()
    meta_left()
    pltpu.make_async_copy(ret_send.at[most], ret_got.at[most], ret_sems.at[0]).wait()
    for c in range(CHUNKS):
        rows = pl.ds(c * CHUNK, CHUNK)
        for dst in range(SLOTS):
            if (dst, c) in ((0, 0), (0, 1), (1, 3), (2, 2)):
                continue
            sent = pltpu.make_async_copy(parts.at[0, rows], parts.at[dst, rows], copy_send.at[dst, c])
            if (dst, c) in ((2, 0), (2, 1)):
                pl.when((x + 4 - step) % 4 < 2)(sent.wait)
            else:
                sent.wait()
    for dst in range(1, SLOTS):
        pltpu.make_async_copy(clr.at[0], clr.at[dst], cl_send.at[dst]).wait()
        pltpu.make_async_copy(acc.at[dst], acc_got.at[dst - 1], acc_send.at[dst]).wait()


def per_device(embeddings, sorted_pos, block_cluster, tile_list):
    del tile_list
    vmem = pl.BlockSpec(memory_space=pltpu.VMEM)
    out = pl.pallas_call(
        kernel,
        out_shape=jax.ShapeDtypeStruct((1, ROWS), F32),
        in_specs=[pl.BlockSpec(memory_space=pl.ANY), vmem, pl.BlockSpec(memory_space=pltpu.SMEM)],
        out_specs=vmem,
        scratch_shapes=[
            pltpu.VMEM((ROWS, D), BF16),
            pltpu.VMEM((ROWS, D), BF16),
            pltpu.VMEM((ROWS, 128), F32),
            pltpu.VMEM((DEVS, PAIR, D), BF16),
            pltpu.VMEM((4, DEVS // 4, PAIR, D), BF16),
            pltpu.VMEM((SLOTS, ROWS, D), BF16),
            pltpu.VMEM((8, 128), F32),
            pltpu.VMEM((8, 128), F32),
            pltpu.VMEM((8, ROWS), F32),
            pltpu.VMEM((SLOTS, 8, ROWS), F32),
            pltpu.VMEM((SLOTS, ROWS, 128), F32),
            pltpu.VMEM((SLOTS, 8, ROWS), F32),
            pltpu.VMEM((SLOTS - 1, 8, ROWS), F32),
            pltpu.VMEM((8, 16, 1, 128), F32),
            pltpu.VMEM((8, 16, 1, 128), F32),
            pltpu.VMEM((16, 8, 1, 128), F32),
            pltpu.VMEM((DEVS, 1, 128), F32),
            pltpu.VMEM((DEVS, 1, 128), F32),
            pltpu.VMEM((1, ROWS), jnp.int32),
            pltpu.VMEM((128, ROWS), BF16),
            pltpu.VMEM((DEVS, ROWS), F32),
            pltpu.SemaphoreType.DMA,
            pltpu.SemaphoreType.DMA((4,)),
            pltpu.SemaphoreType.DMA((2,)),
            pltpu.SemaphoreType.DMA((SLOTS, CHUNKS)),
            pltpu.SemaphoreType.DMA((SLOTS, CHUNKS)),
            pltpu.SemaphoreType.DMA((SLOTS,)),
            pltpu.SemaphoreType.DMA((SLOTS,)),
            pltpu.SemaphoreType.DMA((SLOTS,)),
            pltpu.SemaphoreType.DMA((SLOTS,)),
            pltpu.SemaphoreType.DMA((2,)),
            pltpu.SemaphoreType.DMA((4,)),
            pltpu.SemaphoreType.DMA((4,)),
            pltpu.SemaphoreType.DMA,
            pltpu.SemaphoreType.DMA((2,)),
        ],
        compiler_params=pltpu.CompilerParams(
            collective_id=0, has_side_effects=True, vmem_limit_bytes=56 * 1024 * 1024
        ),
    )(embeddings, sorted_pos.reshape(1, ROWS), block_cluster)
    return out.reshape(ROWS)


def solution(mesh):
    placed = (
        P(("owner", "tile"), None),
        P(("owner", "tile")),
        P(("owner", "tile")),
        P("owner", "tile", None, None),
    )
    return jax.shard_map(
        per_device, mesh=mesh, in_specs=placed, out_specs=P(("owner", "tile")), check_vma=False
    )
```
